512 devices in a mesh: segment: 4 (over x), grp: 16 (over y, z_hi), sp: 8 (over z_lo, core).
Axes of the slice: x: 4, y: 8, z: 8 (z_hi: 2, z_lo: 4; z = z_hi * 4 + z_lo), core: 2. Of those that a mesh axis runs over, the one named last changes fastest.
Arguments:
- queries: bfloat16 [4, 16, 4, 32, 16, 2048], P('segment', 'grp', None, 'sp'), may hold values from -140 to 140
- key_states: bfloat16 [4, 16, 4, 32, 16, 2048], P('segment', 'grp', None, 'sp'), may hold values from -6 to 6
- value_states: bfloat16 [4, 16, 4, 32, 16, 2048], P('segment', 'grp', None, 'sp'), may hold values from -6 to 6
- kept_tiles: int32 [16, 8, 4], replicated, may hold values from 0 to 7, as said below
- kept_counts: int32 [16, 8], replicated, may hold values from 1 to 4
- patch_weight: bfloat16 [2048, 64], replicated, may hold values from -1.5 to 1.5
- decode_slot: int32 [4], replicated, may hold values from 0 to 3, each once
- first_kernel: bfloat16 [27, 16, 256], replicated, may hold values from -0.3125 to 0.3125
- second_kernel: bfloat16 [27, 256, 256], P(None, 'grp'), may hold values from -0.078125 to 0.078125
Outputs:
- decoded: bfloat16 [4, 16, 4, 64, 32, 256], P('segment', 'grp', None, 'sp')
The draws below stay inside these ranges and needn't reach their ends.
Inputs may be any that keep to these rules, and one draw needn't show every extreme that they name: `kept_tiles`: for each head and query tile the 4 entries name distinct tiles, the query tile itself among them in some slot.
All inputs are finite; a program needn't handle non-finite values.
Results may differ from the reference program's by a relative error of at most 0.018.
Values may be sent and summed in bfloat16 or wider, within the bound.
A program may use at most 128 MiB of HBM per device.

```python
import jax
import jax.numpy as jnp
from jax import lax

HEADS = 16
HD = 128
LAT = 16
CH = 256
TT = 4
TH = 8
TW = 8
FT = 4
FW = 16
FH = 32
TILE = 256
SEQ = 2048
NT = 8
KEEP = 4
MICRO = 4
CLIPS = 16


def grid_shape():
    return (MICRO, CLIPS, FT, FH, FW, HEADS * HD)


def shared_keys(key):
    return jax.random.truncated_normal(jax.random.fold_in(key, 7), -6.0, 6.0, grid_shape(), jnp.float32)


def draw_key_states(key, part):
    base = shared_keys(key)
    return base.astype(jnp.bfloat16)


def draw_queries(key, part):
    base = shared_keys(key)
    key = jax.random.fold_in(key, 5)
    result = jax.random.truncated_normal(jax.random.fold_in(key, 2), -6.0, 6.0, base.shape, jnp.float32)
    return result.astype(jnp.bfloat16)


def draw_kept_tiles(key, part):
    key = jax.random.fold_in(key, 11)
    noise = jax.random.randint(jax.random.fold_in(key, 1), (HEADS, NT, NT), 0, 1 << 20)
    column = jnp.arange(NT, dtype=jnp.int32)
    ranked = noise * NT + column[None, None, :]
    ranked = jnp.where(column[None, None, :] == column[None, :, None], -1, ranked)
    order = jnp.argsort(ranked, axis=-1, stable=True)[:, :, :KEEP]
    slot_noise = jax.random.randint(jax.random.fold_in(key, 2), (HEADS, NT, KEEP), 0, 1 << 20)
    slot_rank = slot_noise * KEEP + jnp.arange(KEEP, dtype=jnp.int32)[None, None, :]
    shuffle = jnp.argsort(slot_rank, axis=-1, stable=True)
    return jnp.take_along_axis(order, shuffle, axis=-1).astype(jnp.int32)


def draw_kept_counts(key, part):
    key = jax.random.fold_in(key, 13)
    level = jax.random.randint(jax.random.fold_in(key, 1), (HEADS, 1), 1, KEEP + 1)
    counts = jax.random.randint(jax.random.fold_in(key, 2), (HEADS, NT), 1, level + 1)
    chosen_spot = jax.random.randint(jax.random.fold_in(key, 3), (), 0, HEADS * NT)
    flat_counts = jnp.where(jnp.arange(HEADS * NT) == chosen_spot, KEEP, counts.reshape(-1))
    return flat_counts.reshape(HEADS, NT).astype(jnp.int32)


def shard_levels(stream_key, shape, cuts, low, largest):
    gain = 1.0
    for position, parts in cuts:
        draws = jax.random.uniform(jax.random.fold_in(jax.random.fold_in(stream_key, 6), position), (parts,), jnp.float32, low / len(cuts), largest / len(cuts))
        gain = gain * jnp.repeat(jnp.exp(draws), shape[position] // parts).reshape((-1,) + (1,) * (len(shape) - 1 - position))
    return gain


def centred(key, dims, spread, bound, split=(), kind=jnp.bfloat16):
    drawn = spread * jax.random.normal(key, dims, jnp.float32)
    if split:
        drawn = drawn * shard_levels(key, dims, split, -0.22, 0.18)
    return jnp.clip(drawn, -bound, bound).astype(kind)


def setup_inputs(seed: int = 0) -> dict:
    seeds = jax.random.split(jax.random.key(seed), 10)
    queries = draw_queries(jax.random.fold_in(seeds[9], 71), 0)
    key_states = draw_key_states(jax.random.fold_in(seeds[9], 71), 0)
    value_states = centred(seeds[2], (MICRO, CLIPS, FT, FH, FW, HEADS * HD), 1.0, 6.0, ((0, 4), (1, 16), (3, 8)))
    kept_tiles = draw_kept_tiles(jax.random.fold_in(seeds[9], 71), 0)
    kept_counts = draw_kept_counts(jax.random.fold_in(seeds[9], 71), 0)
    patch_weight = centred(seeds[5], (HEADS * HD, 4 * LAT), 16 ** -0.5, 1.5)
    decode_slot = jax.random.permutation(seeds[6], MICRO).astype(jnp.int32)
    first_kernel = centred(seeds[7], (27, LAT, CH), (27 * LAT) ** -0.5, 0.3125)
    second_kernel = centred(seeds[8], (27, CH, CH), (27 * CH) ** -0.5, 0.078125, ((1, 16),))
    return {"queries": queries, "key_states": key_states, "value_states": value_states, "kept_tiles": kept_tiles, "kept_counts": kept_counts, "patch_weight": patch_weight, "decode_slot": decode_slot, "first_kernel": first_kernel, "second_kernel": second_kernel}


VAE_SCALE = 1.0 / 0.476986


def head_attention(packed):
    query_tiles, key_tiles, value_tiles, tile_index, live_count = packed
    key_sel = key_tiles[tile_index].reshape(NT, KEEP * TILE, HD)
    value_sel = value_tiles[tile_index].reshape(NT, KEEP * TILE, HD)
    scores = jnp.einsum('nqd,nkd->nqk', query_tiles.astype(jnp.float32), key_sel.astype(jnp.float32)) * (HD ** -0.5)
    live = jnp.arange(KEEP, dtype=jnp.int32)[None, :] < live_count[:, None]
    live = jnp.repeat(live, TILE, axis=1)[:, None, :]
    scores = jnp.where(live, scores, -1e30)
    row_top = jnp.max(scores, axis=-1, keepdims=True)
    exponent = jnp.where(live, jnp.exp(scores - row_top), 0.0)
    weights = (exponent / jnp.sum(exponent, axis=-1, keepdims=True)).astype(jnp.bfloat16)
    result = jnp.einsum('nqk,nkd->nqd', weights.astype(jnp.float32), value_sel.astype(jnp.float32))
    return result.astype(jnp.bfloat16)


def to_tiles(grid):
    feature_width = grid.shape[-1]
    tiled = grid.reshape(FT // TT, TT, FH // TH, TH, FW // TW, TW, feature_width).transpose(0, 2, 4, 1, 3, 5, 6)
    return tiled.reshape(NT, TILE, feature_width)


def from_tiles(tiles):
    feature_width = tiles.shape[-1]
    grid = tiles.reshape(FT // TT, FH // TH, FW // TW, TT, TH, TW, feature_width).transpose(0, 3, 1, 4, 2, 5, 6)
    return grid.reshape(FT, FH, FW, feature_width)


def split_heads(tiles):
    return tiles.reshape(NT, TILE, HEADS, HD).transpose(2, 0, 1, 3)


def clip_latent(query_clip, key_clip, value_clip, kept_tiles, kept_counts, patch_weight):
    packed = (split_heads(to_tiles(query_clip)), split_heads(to_tiles(key_clip)), split_heads(to_tiles(value_clip)), kept_tiles, kept_counts)
    outputs = lax.map(head_attention, packed)
    attended = from_tiles(outputs.transpose(1, 2, 0, 3).reshape(NT, TILE, HEADS * HD))
    latent = jnp.dot(attended.reshape(SEQ, HEADS * HD), patch_weight, preferred_element_type=jnp.float32).astype(jnp.bfloat16)
    return latent.reshape(FT, FH, FW, 4 * LAT)


def to_cells(latent):
    grid = latent.reshape(FT, FH, FW, 2, 2, LAT).transpose(0, 1, 3, 2, 4, 5)
    return grid.reshape(FT, 2 * FH, 2 * FW, LAT)


def convolve(cells, kernel):
    row_count = cells.shape[1]
    col_count = cells.shape[2]
    padded = jnp.pad(cells, ((2, 0), (1, 1), (1, 1), (0, 0)), mode='edge')
    total = jnp.zeros((FT * row_count * col_count, kernel.shape[2]), jnp.float32)
    for offset_time in range(3):
        for offset_row in range(3):
            for offset_col in range(3):
                window = padded[offset_time:offset_time + FT, offset_row:offset_row + row_count, offset_col:offset_col + col_count]
                total = total + jnp.dot(window.reshape(-1, cells.shape[3]), kernel[(offset_time * 3 + offset_row) * 3 + offset_col], preferred_element_type=jnp.float32)
    return total.reshape(FT, row_count, col_count, kernel.shape[2])


def decode_clip(latent, first_kernel, second_kernel):
    cells = to_cells(latent)
    first = (convolve(cells, first_kernel) * VAE_SCALE).astype(jnp.bfloat16)
    act = jax.nn.silu(first.astype(jnp.float32)).astype(jnp.bfloat16)
    return (first.astype(jnp.float32) + convolve(act, second_kernel)).astype(jnp.bfloat16)


def reference(queries, key_states, value_states, kept_tiles, kept_counts, patch_weight, decode_slot, first_kernel, second_kernel):
    def flatten(block):
        return block.reshape(MICRO * CLIPS, FT, FH, FW, HEADS * HD)

    def one_clip(packed):
        return clip_latent(packed[0], packed[1], packed[2], kept_tiles, kept_counts, patch_weight)

    latents = lax.map(one_clip, (flatten(queries), flatten(key_states), flatten(value_states)))
    latents = latents.reshape(MICRO, CLIPS, FT, FH, FW, 4 * LAT)
    match = (decode_slot[:, None] == jnp.arange(MICRO, dtype=jnp.int32)[None, :]).astype(jnp.int32)
    source = jnp.sum(jnp.arange(MICRO, dtype=jnp.int32)[:, None] * match, axis=0).astype(jnp.int32)
    moved = latents[source].reshape(MICRO * CLIPS, FT, FH, FW, 4 * LAT)

    def one_decode(latent):
        return decode_clip(latent, first_kernel, second_kernel)

    decoded = lax.map(one_decode, moved)
    return decoded.reshape(MICRO, CLIPS, FT, 2 * FH, 2 * FW, CH)
```

```python
import functools
import math

import jax
import jax.numpy as jnp
from jax import lax
from jax.experimental import pallas as pl
from jax.experimental.pallas import tpu as pltpu
from jax.sharding import PartitionSpec as P

HEADS = 16
HD = 128
LAT = 16
CH = 256
NT = 8
KEEP = 4
TILE = 256
VAE_SCALE = 1.0 / 0.476986
MESH = pl.DeviceIdType.MESH
BF16 = jnp.bfloat16
F32 = jnp.float32
EXPONENT_SCALE = HD**-0.5 * math.log2(math.e)


def remote(src, dst, send_sem, recv_sem, **where):
    return pltpu.make_async_remote_copy(
        src_ref=src,
        dst_ref=dst,
        send_sem=send_sem,
        recv_sem=recv_sem,
        device_id=where,
        device_id_type=MESH,
    )


def exchange_kernel(
    kept,
    counts,
    decode_slot,
    queries,
    keys,
    values,
    patch,
    piece,
    latent_out,
    weights_out,
    got_q,
    got_k,
    got_v,
    tile_q,
    tile_k,
    tile_v,
    order,
    patch_own,
    attended,
    part_out,
    part_in,
    seg_latent,
    send_sem,
    recv_sem,
    local_sem,
    part_send,
    part_recv,
    seg_send,
    seg_recv,
    w_local,
    w_send,
    w_recv,
):
    me = lax.axis_index("sp")
    seg = lax.axis_index("segment")
    grp = lax.axis_index("grp")
    chip = me // 2
    core = me % 2
    sibling = chip * 2 + 1 - core
    far = (chip + 2) % 4
    mirror = 3 - chip
    near = chip + 1 - 2 * (chip % 2)
    peers = [
        far * 2 + core,
        far * 2 + 1 - core,
        mirror * 2 + core,
        mirror * 2 + 1 - core,
        near * 2 + core,
        near * 2 + 1 - core,
        sibling,
    ]
    z_partner = grp + 1 - 2 * (grp % 2)
    y_peers = [(grp + 2 * step) % 16 for step in range(1, 8)]
    x_peers = [(seg + step) % 4 for step in range(1, 4)]

    barrier = pltpu.get_barrier_semaphore()
    for peer in peers:
        pl.semaphore_signal(barrier, inc=1, device_id={"sp": peer}, device_id_type=MESH)
    for peer in x_peers:
        pl.semaphore_signal(barrier, inc=1, device_id={"segment": peer}, device_id_type=MESH)
    for peer in [z_partner] + y_peers:
        pl.semaphore_signal(barrier, inc=1, device_id={"grp": peer}, device_id_type=MESH)
    pl.semaphore_wait(barrier, 18)

    quarter = seg * 7
    taps = pl.ds(quarter, 7)
    lanes = pl.ds(pl.multiple_of(core * 128, 128), 128)
    own_part = piece.at[pl.ds(quarter - seg // 3, 7), :, lanes]
    own_rows = pl.ds(pl.multiple_of(grp * 16, 16), 16)
    w_keep = pltpu.make_async_copy(own_part, weights_out.at[taps, own_rows, lanes], w_local)
    w_keep.start()
    w_cross = remote(
        own_part, weights_out.at[taps, own_rows, lanes], w_send.at[0], w_recv.at[0], grp=z_partner
    )
    w_cross.start()

    arrays = ((keys, got_k), (values, got_v), (queries, got_q))
    sends = []
    for a, (source, target) in enumerate(arrays):
        for i, peer in enumerate(peers):
            columns = pl.ds(pl.multiple_of(peer * 256, 256), 256)
            copy = remote(
                source.at[:, columns],
                target.at[me],
                send_sem.at[a, i],
                recv_sem.at[a, me],
                sp=peer,
            )
            copy.start()
            sends.append(copy)
    own_columns = pl.ds(pl.multiple_of(me * 256, 256), 256)
    keeps = []
    for a, (source, target) in enumerate(arrays):
        copy = pltpu.make_async_copy(source.at[:, own_columns], target.at[me], local_sem.at[a])
        copy.start()
        keeps.append(copy)
    patch_copy = pltpu.make_async_copy(
        patch.at[:, pl.ds(pl.multiple_of(me * 256, 256), 256)], patch_own, local_sem.at[3]
    )
    patch_copy.start()

    w_keep.wait()
    w_cross.wait()
    pair_rows = pl.ds(pl.multiple_of((grp // 2) * 32, 32), 32)
    y_sends = []
    for i, peer in enumerate(y_peers):
        block = weights_out.at[taps, pair_rows, lanes]
        copy = remote(block, block, w_send.at[1 + i], w_recv.at[1 + i], grp=peer)
        copy.start()
        y_sends.append(copy)
    for copy in keeps:
        copy.wait()
    patch_copy.wait()
    for copy in y_sends:
        copy.wait()
    x_sends = []
    own_quarter = weights_out.at[taps, :, lanes]
    for i, peer in enumerate(x_peers):
        copy = remote(own_quarter, own_quarter, w_send.at[8 + i], w_recv.at[8 + i], segment=peer)
        copy.start()
        x_sends.append(copy)

    def wait_block(a, target, src):
        remote(
            target.at[src], target.at[src], send_sem.at[a, 0], recv_sem.at[a, src], sp=sibling
        ).wait_recv()

    to_row = lax.broadcasted_iota(jnp.int32, (256, 256), 0)
    from_row = lax.broadcasted_iota(jnp.int32, (256, 256), 1)
    wanted = ((to_row % 128) // 8) * 16 + (to_row // 128) * 8 + to_row % 8
    order[...] = (from_row == wanted).astype(BF16)

    def place(got, src, tiles, first_tile):
        block = jnp.dot(order[...], got[src], preferred_element_type=F32).astype(BF16)
        rows = pl.ds(pl.multiple_of((src % 2) * 128, 128), 128)
        for head in range(2):
            for side in range(2):
                tiles[head, first_tile + side, rows] = block[
                    side * 128 : side * 128 + 128, head * 128 : head * 128 + 128
                ]

    def place_keys(src):
        place(got_k, src, tile_k, 2 * (src // 2))
        place(got_v, src, tile_v, 2 * (src // 2))

    place_keys(me)
    for peer in (peers[6], peers[4], peers[5]):
        wait_block(0, got_k, peer)
        wait_block(1, got_v, peer)
        place_keys(peer)

    for copy in x_sends:
        copy.wait()
    all_lanes = weights_out.at[:, :, lanes]
    to_sibling = remote(all_lanes, all_lanes, w_send.at[11], w_recv.at[11], sp=sibling)
    to_sibling.start()

    for peer in peers[:4]:
        wait_block(0, got_k, peer)
        wait_block(1, got_v, peer)
        place_keys(peer)

    head_base = me * 2
    zero_patch = jnp.zeros((64, 256), F32)
    own_patch = patch_own[...].astype(F32)
    wide_patch = jnp.concatenate(
        [
            jnp.concatenate([own_patch, zero_patch], axis=1),
            jnp.concatenate([zero_patch, own_patch], axis=1),
        ],
        axis=0,
    ).astype(BF16)

    def one_tile(owner, side):
        tile = 2 * owner + side
        for head in range(2):
            low = head * 128
            query = tile_q[head, side]
            live = counts[tile, head_base + head]
            scores, picks = [], []
            for slot in range(KEEP):
                pick = kept[tile, slot, head_base + head]
                picks.append(pick)
                scores.append(
                    lax.dot_general(
                        query,
                        tile_k[head, pick],
                        (((1,), (1,)), ((), ())),
                        preferred_element_type=F32,
                    )
                )
            top = scores[0]
            for slot in range(1, KEEP):
                top = jnp.maximum(top, jnp.where(slot < live, scores[slot], -1e30))
            top = jnp.max(top, axis=1, keepdims=True) * EXPONENT_SCALE
            total = jnp.zeros((TILE, TILE), F32)
            result = jnp.zeros((TILE, HD), F32)
            for slot in range(KEEP):
                shift = top if slot == 0 else jnp.where(slot < live, top, 1e30)
                exponent = jnp.exp2(scores[slot] * EXPONENT_SCALE - shift)
                total = total + exponent
                result = result + jnp.dot(
                    exponent.astype(BF16), tile_v[head, picks[slot]], preferred_element_type=F32
                )
            total = jnp.sum(total, axis=1, keepdims=True)
            attended[side, :, low : low + 128] = (result / total).astype(BF16)

    def part_targets(owner, half):
        block = 2 * owner + half
        last = block // 7
        start = 1 - (block + 6) // 7
        own = part_out.at[owner, half]
        return (
            (own, block, 32, 128),
            (own.at[pl.ds(96, 32)], block + 1 - last, 160 * last, 32),
            (own.at[pl.ds(0, 32)], block - 1 + start, 160 * (1 - start), 32),
        )

    def one_chip(owner):
        place(got_q, 2 * owner, tile_q, 0)
        place(got_q, 2 * owner + 1, tile_q, 0)
        one_tile(owner, 0)
        one_tile(owner, 1)
        stacked = []
        for half in range(2):
            for side in range(2):
                base = half * 128
                stacked.append(
                    jnp.concatenate(
                        [
                            attended[side, base : base + 64],
                            attended[side, base + 64 : base + 128],
                        ],
                        axis=1,
                    )
                )
        projected = lax.dot_general(
            jnp.concatenate(stacked, axis=0),
            wide_patch,
            (((1,), (1,)), ((), ())),
            preferred_element_type=F32,
        )
        for half in range(2):
            pieces = []
            for row in range(4):
                for frame in range(2):
                    for side in range(2):
                        at = ((half * 2 + side) * 8 + frame * 4 + row) * 8
                        pieces.append(projected[at : at + 8])
            part_out[owner, half] = jnp.concatenate(pieces, axis=0).astype(BF16)
        for half in range(2):
            for kind, (source, target, at, size) in enumerate(part_targets(owner, half)):
                place_at = part_in.at[me, pl.ds(pl.multiple_of(at, 32), size)]

                @pl.when(target != me)
                def _():
                    remote(
                        source,
                        place_at,
                        part_send.at[owner, half, kind],
                        part_recv.at[me],
                        sp=target,
                    ).start()

                @pl.when(target == me)
                def _():
                    pltpu.make_async_copy(source, place_at, part_recv.at[me]).start()

    def chip_turn(turn, carry):
        owner = (
            (turn == 0) * chip + (turn == 1) * near + (turn == 2) * far + (turn == 3) * mirror
        )

        @pl.when(turn > 0)
        def _():
            for k in range(2):
                wait_block(2, got_q, owner * 2 + k)

        one_chip(owner)
        return carry

    wait_block(2, got_q, sibling)
    lax.fori_loop(0, 4, chip_turn, 0)

    for src in range(8):
        pltpu.make_async_copy(part_in.at[src], part_in.at[src], part_recv.at[src]).wait()
    latent = jnp.zeros((192, 128), F32)
    for src in range(8):
        latent = latent + part_in[src].astype(F32)
    seg_latent[seg] = latent.astype(BF16)
    seg_copies = []
    for i, peer in enumerate(x_peers):
        copy = remote(
            seg_latent.at[seg], seg_latent.at[seg], seg_send.at[i], seg_recv.at[i], segment=peer
        )
        copy.start()
        seg_copies.append(copy)
    for copy in seg_copies:
        copy.wait()
    source = jnp.int32(0)
    for micro in range(1, 4):
        source = jnp.where(decode_slot[micro] == seg, micro, source)
    latent_out[...] = seg_latent[source]

    def drain(owner, carry):
        for half in range(2):
            for kind, (source, target, at, size) in enumerate(part_targets(owner, half)):

                @pl.when(target != me)
                def _():
                    remote(
                        source,
                        part_in.at[me, pl.ds(0, size)],
                        part_send.at[owner, half, kind],
                        part_recv.at[me],
                        sp=target,
                    ).wait_send()

        return carry

    lax.fori_loop(0, 4, drain, 0)
    to_sibling.wait()
    for copy in sends:
        copy.wait_send()


def exchange(kept, counts, decode_slot, queries, keys, values, patch, piece):
    any_space = pl.BlockSpec(memory_space=pl.ANY)
    smem = pl.BlockSpec(memory_space=pltpu.SMEM)
    vmem = pl.BlockSpec(memory_space=pltpu.VMEM)
    return pl.pallas_call(
        exchange_kernel,
        out_shape=(
            jax.ShapeDtypeStruct((192, 128), BF16),
            jax.ShapeDtypeStruct((28, CH, CH), BF16),
        ),
        in_specs=[smem, smem, smem] + [any_space] * 5,
        out_specs=(vmem, any_space),
        scratch_shapes=[
            pltpu.VMEM((8, 256, 256), BF16),
            pltpu.VMEM((8, 256, 256), BF16),
            pltpu.VMEM((8, 256, 256), BF16),
            pltpu.VMEM((2, 2, TILE, HD), BF16),
            pltpu.VMEM((2, NT, TILE, HD), BF16),
            pltpu.VMEM((2, NT, TILE, HD), BF16),
            pltpu.VMEM((256, 256), BF16),
            pltpu.VMEM((64, 256), BF16),
            pltpu.VMEM((2, TILE, 256), BF16),
            pltpu.VMEM((4, 2, 128, 128), BF16),
            pltpu.VMEM((8, 192, 128), BF16),
            pltpu.VMEM((4, 192, 128), BF16),
            pltpu.SemaphoreType.DMA((3, 7)),
            pltpu.SemaphoreType.DMA((3, 8)),
            pltpu.SemaphoreType.DMA((4,)),
            pltpu.SemaphoreType.DMA((4, 2, 3)),
            pltpu.SemaphoreType.DMA((8,)),
            pltpu.SemaphoreType.DMA((3,)),
            pltpu.SemaphoreType.DMA((3,)),
            pltpu.SemaphoreType.DMA,
            pltpu.SemaphoreType.DMA((12,)),
            pltpu.SemaphoreType.DMA((12,)),
        ],
        compiler_params=pltpu.CompilerParams(
            collective_id=0, has_side_effects=True, vmem_limit_bytes=60 << 20
        ),
        cost_estimate=pl.CostEstimate(
            flops=4 * 16 * 4 * 256 * 256 * 128, bytes_accessed=10 << 20, transcendentals=1 << 22
        ),
    )(kept, counts, decode_slot, queries, keys, values, patch, piece)


def slot_of(offset):
    return offset if offset < 21 else offset + 1


def decode_kernel(
    latent, first_kernel, weights, out, window, first, act, weights_vmem, weight_sem
):
    me = lax.axis_index("sp")
    load = pltpu.make_async_copy(weights, weights_vmem, weight_sem)
    load.start()

    twice = (
        lax.broadcasted_iota(jnp.int32, (384, 192), 0) // 2
        == lax.broadcasted_iota(jnp.int32, (384, 192), 1)
    ).astype(BF16)
    doubled = jnp.dot(twice, latent[...], preferred_element_type=F32)
    column = lax.broadcasted_iota(jnp.int32, (384, 128), 0) % 32
    here = jnp.where(column % 2 == 0, doubled, pltpu.roll(doubled, 128 - LAT, axis=1))
    before = jnp.where(column == 0, here, pltpu.roll(here, 1, axis=0))
    after = jnp.where(column == 31, here, pltpu.roll(here, 383, axis=0))
    source_lane = lax.broadcasted_iota(jnp.int32, (384, 512), 0)
    target_lane = lax.broadcasted_iota(jnp.int32, (384, 512), 1)
    slot = target_lane % 128
    wanted = (slot // LAT) * 128 + (target_lane // 128) * 32 + slot % LAT
    pick = jnp.logical_and(slot < 48, source_lane == wanted).astype(BF16)
    joined = jnp.dot(
        jnp.concatenate([before, here, after], axis=1).astype(BF16),
        pick,
        preferred_element_type=F32,
    ).astype(BF16)
    for row in range(6):
        for frame_low in range(2):
            at = (row * 2 + frame_low) * 32
            for frame_high in range(2):
                for up in range(2):
                    lane = (frame_high * 2 + up) * 128
                    window[frame_high * 2 + frame_low, 2 * row + up] = joined[
                        at : at + 32, lane : lane + 128
                    ]

    @pl.when(me == 0)
    def _():
        window[:, 1] = window[:, 2]

    @pl.when(me == 7)
    def _():
        window[:, 10] = window[:, 9]

    wide_column = lax.broadcasted_iota(jnp.int32, (320, CH), 0) % 32
    for frame in range(4):
        total = jnp.zeros((320, CH), F32)
        for time in range(3):
            source = max(frame + time - 2, 0)
            for row in range(3):
                offset = (time * 3 + row) * 48
                total = total + jnp.dot(
                    window[source, row : row + 10, :, 0:48].reshape(320, 48),
                    first_kernel[offset : offset + 48],
                    preferred_element_type=F32,
                )
        rounded = (total * VAE_SCALE).astype(BF16)
        first[frame * 256 : frame * 256 + 256] = rounded[32:288]
        wide = rounded.astype(F32)
        wide = (wide / (1.0 + jnp.exp(-wide))).astype(BF16).astype(F32)
        before = jnp.where(wide_column == 0, wide, pltpu.roll(wide, 1, axis=0))
        after = jnp.where(wide_column == 31, wide, pltpu.roll(wide, 319, axis=0))
        for place, part in enumerate((before, wide, after)):
            part = part.reshape(10, 32, CH).astype(BF16)
            act[frame + 2, :, :, place * CH : place * CH + CH] = part
            if frame == 0:
                act[0, :, :, place * CH : place * CH + CH] = part
                act[1, :, :, place * CH : place * CH + CH] = part

    @pl.when(me == 0)
    def _():
        act[:, 0] = act[:, 1]

    @pl.when(me == 7)
    def _():
        act[:, 9] = act[:, 8]

    load.wait()
    for part in range(2):
        total = first[part * 512 : part * 512 + 512].astype(F32)
        for time in range(3):
            for row in range(3):
                slot = slot_of((time * 3 + row) * 3)
                block = act[part * 2 + time : part * 2 + time + 2, row : row + 8]
                total = total + jnp.dot(
                    block.reshape(512, 3 * CH),
                    weights_vmem[slot : slot + 3].reshape(3 * CH, CH),
                    preferred_element_type=F32,
                )
        out[part * 512 : part * 512 + 512] = total.astype(BF16)


def decode(latent, first_kernel, weights):
    vmem = pl.BlockSpec(memory_space=pltpu.VMEM)
    return pl.pallas_call(
        decode_kernel,
        out_shape=jax.ShapeDtypeStruct((1024, CH), BF16),
        in_specs=[vmem, vmem, pl.BlockSpec(memory_space=pl.ANY)],
        out_specs=vmem,
        scratch_shapes=[
            pltpu.VMEM((4, 12, 32, 128), BF16),
            pltpu.VMEM((1024, CH), BF16),
            pltpu.VMEM((6, 10, 32, 3 * CH), BF16),
            pltpu.VMEM((28, CH, CH), BF16),
            pltpu.SemaphoreType.DMA,
        ],
        compiler_params=pltpu.CompilerParams(vmem_limit_bytes=40 << 20),
        cost_estimate=pl.CostEstimate(
            flops=2 * 1024 * 27 * 256 * 256, bytes_accessed=5 << 20, transcendentals=1 << 19
        ),
    )(latent, first_kernel, weights)


def local(
    queries,
    key_states,
    value_states,
    kept_tiles,
    kept_counts,
    patch_weight,
    decode_slot,
    first_kernel,
    second_kernel,
):
    latent, weights = exchange(
        kept_tiles.transpose(1, 2, 0),
        kept_counts.transpose(1, 0),
        decode_slot,
        queries.reshape(256, HEADS * HD),
        key_states.reshape(256, HEADS * HD),
        value_states.reshape(256, HEADS * HD),
        patch_weight.transpose(1, 0),
        second_kernel,
    )
    decoded = decode(latent, first_kernel.reshape(27 * LAT, CH), weights)
    return decoded.reshape(1, 1, 4, 8, 32, CH)


def solution(mesh):
    tokens = P("segment", "grp", None, "sp", None, None)
    return jax.shard_map(
        local,
        mesh=mesh,
        in_specs=(tokens, tokens, tokens, P(), P(), P(), P(), P(), P(None, "grp", None)),
        out_specs=tokens,
        check_vma=False,
    )
```

```python
import functools
import math

import jax
import jax.numpy as jnp
from jax import lax
from jax.experimental import pallas as pl
from jax.experimental.pallas import tpu as pltpu
from jax.sharding import PartitionSpec as P

HEADS = 16
HD = 128
LAT = 16
CH = 256
NT = 8
KEEP = 4
TILE = 256
VAE_SCALE = 1.0 / 0.476986
MESH = pl.DeviceIdType.MESH
BF16 = jnp.bfloat16
F32 = jnp.float32
EXPONENT_SCALE = HD**-0.5 * math.log2(math.e)


def remote(src, dst, send_sem, recv_sem, **where):
    return pltpu.make_async_remote_copy(
        src_ref=src,
        dst_ref=dst,
        send_sem=send_sem,
        recv_sem=recv_sem,
        device_id=where,
        device_id_type=MESH,
    )


def exchange_kernel(
    kept,
    counts,
    decode_slot,
    queries,
    keys,
    values,
    patch,
    piece,
    latent_out,
    weights_out,
    got_q,
    got_k,
    got_v,
    tile_q,
    tile_k,
    tile_v,
    order,
    patch_all,
    own_values,
    projected,
    packed,
    part_out,
    sib_in,
    part_sum,
    part_in,
    seg_latent,
    send_sem,
    recv_sem,
    local_sem,
    sib_send,
    sib_recv,
    part_send,
    part_recv,
    seg_send,
    seg_recv,
    w_local,
    w_send,
    w_recv,
):
    me = lax.axis_index("sp")
    seg = lax.axis_index("segment")
    grp = lax.axis_index("grp")
    chip = me // 2
    core = me % 2
    sibling = chip * 2 + 1 - core
    far = (chip + 2) % 4
    mirror = 3 - chip
    near = chip + 1 - 2 * (chip % 2)
    peers = [
        far * 2 + core,
        far * 2 + 1 - core,
        mirror * 2 + core,
        mirror * 2 + 1 - core,
        near * 2 + core,
        near * 2 + 1 - core,
        sibling,
    ]
    z_partner = grp + 1 - 2 * (grp % 2)
    y_peers = [(grp + 2 * step) % 16 for step in range(1, 8)]
    x_peers = [(seg + step) % 4 for step in range(1, 4)]

    barrier = pltpu.get_barrier_semaphore()
    for peer in peers:
        pl.semaphore_signal(barrier, inc=1, device_id={"sp": peer}, device_id_type=MESH)
    for peer in x_peers:
        pl.semaphore_signal(barrier, inc=1, device_id={"segment": peer}, device_id_type=MESH)
    for peer in [z_partner] + y_peers:
        pl.semaphore_signal(barrier, inc=1, device_id={"grp": peer}, device_id_type=MESH)
    pl.semaphore_wait(barrier, 18)

    sends = []

    def send(a, source, target):
        for i, peer in enumerate(peers):
            copy = remote(source(peer), target.at[me], send_sem.at[a, i], recv_sem.at[a, me], sp=peer)
            copy.start()
            sends.append(copy)

    def columns_of(ref):
        return lambda peer: ref.at[:, pl.ds(pl.multiple_of(peer * 256, 256), 256)]

    load_values = pltpu.make_async_copy(values, own_values, local_sem.at[0])
    load_values.start()
    load_patch = pltpu.make_async_copy(patch, patch_all, local_sem.at[1])
    load_patch.start()
    send(0, columns_of(keys), got_k)
    keep_keys = pltpu.make_async_copy(columns_of(keys)(me), got_k.at[me], local_sem.at[2])
    keep_keys.start()
    keep_queries = pltpu.make_async_copy(columns_of(queries)(me), got_q.at[me], local_sem.at[3])
    keep_queries.start()

    quarter = seg * 7
    taps = pl.ds(quarter, 7)
    lanes = pl.ds(pl.multiple_of(core * 128, 128), 128)
    own_part = piece.at[pl.ds(quarter - seg // 3, 7), :, lanes]
    own_rows = pl.ds(pl.multiple_of(grp * 16, 16), 16)
    w_keep = pltpu.make_async_copy(own_part, weights_out.at[taps, own_rows, lanes], w_local)
    w_keep.start()
    w_cross = remote(
        own_part, weights_out.at[taps, own_rows, lanes], w_send.at[0], w_recv.at[0], grp=z_partner
    )
    w_cross.start()

    load_values.wait()
    load_patch.wait()
    patch_lane = lax.broadcasted_iota(jnp.int32, (64, 256), 1)

    def project(peer, carry):
        columns = pl.ds(pl.multiple_of(peer * 256, 256), 256)
        weight = patch_all[:, columns].astype(F32)
        weight = jnp.concatenate(
            [jnp.where(patch_lane < HD, weight, 0.0), jnp.where(patch_lane < HD, 0.0, weight)],
            axis=0,
        ).astype(BF16)
        projected[peer] = lax.dot_general(
            own_values[:, columns],
            weight,
            (((1,), (1,)), ((), ())),
            preferred_element_type=F32,
        ).astype(BF16)
        return carry

    lax.fori_loop(0, 8, project, 0)
    send(1, lambda peer: projected.at[peer], got_v)
    got_v[me] = projected[me]
    send(2, columns_of(queries), got_q)

    w_keep.wait()
    w_cross.wait()
    pair_rows = pl.ds(pl.multiple_of((grp // 2) * 32, 32), 32)
    y_sends = []
    for i, peer in enumerate(y_peers):
        block = weights_out.at[taps, pair_rows, lanes]
        copy = remote(block, block, w_send.at[1 + i], w_recv.at[1 + i], grp=peer)
        copy.start()
        y_sends.append(copy)
    keep_keys.wait()
    keep_queries.wait()
    def wait_block(a, target, src):
        remote(
            target.at[src], target.at[src], send_sem.at[a, 0], recv_sem.at[a, src], sp=sibling
        ).wait_recv()

    to_row = lax.broadcasted_iota(jnp.int32, (256, 256), 0)
    from_row = lax.broadcasted_iota(jnp.int32, (256, 256), 1)
    wanted = ((to_row % 128) // 8) * 16 + (to_row // 128) * 8 + to_row % 8
    order[...] = (from_row == wanted).astype(BF16)

    def place(got, src, tiles, first_tile):
        block = jnp.dot(order[...], got[src], preferred_element_type=F32).astype(BF16)
        rows = pl.ds(pl.multiple_of((src % 2) * 128, 128), 128)
        for head in range(2):
            for side in range(2):
                tiles[head, first_tile + side, rows] = block[
                    side * 128 : side * 128 + 128, head * 128 : head * 128 + 128
                ]

    value_lane = lax.broadcasted_iota(jnp.int32, (256, 128), 1)

    def place_keys(src):
        place(got_k, src, tile_k, 2 * (src // 2))
        block = jnp.dot(order[...], got_v[src], preferred_element_type=F32)
        turned = pltpu.roll(block, 64, axis=1)
        rows = pl.ds(pl.multiple_of((src % 2) * 128, 128), 128)
        for head, (left, right) in enumerate(((block, turned), (turned, block))):
            both = jnp.where(value_lane < 64, left, right).astype(BF16)
            for side in range(2):
                tile_v[head, 2 * (src // 2) + side, rows] = both[side * 128 : side * 128 + 128]

    place_keys(me)
    for peer in (peers[6], peers[4], peers[5]):
        wait_block(0, got_k, peer)
        wait_block(1, got_v, peer)
        place_keys(peer)

    for copy in y_sends:
        copy.wait()
    x_sends = []
    own_quarter = weights_out.at[taps, :, lanes]
    for i, peer in enumerate(x_peers):
        copy = remote(own_quarter, own_quarter, w_send.at[8 + i], w_recv.at[8 + i], segment=peer)
        copy.start()
        x_sends.append(copy)

    for peer in peers[:4]:
        wait_block(0, got_k, peer)
        wait_block(1, got_v, peer)
        place_keys(peer)

    head_base = me * 2
    packed_lane = lax.broadcasted_iota(jnp.int32, (64, 128), 1)

    def one_tile(owner, side):
        tile = 2 * owner + side
        latent = jnp.zeros((TILE, 128), F32)
        for head in range(2):
            query = tile_q[head, side]
            live = counts[tile, head_base + head]
            scores, picks = [], []
            for slot in range(KEEP):
                pick = kept[tile, slot, head_base + head]
                picks.append(pick)
                scores.append(
                    lax.dot_general(
                        query,
                        tile_k[head, pick],
                        (((1,), (1,)), ((), ())),
                        preferred_element_type=F32,
                    )
                )
            top = scores[0]
            for slot in range(1, KEEP):
                top = jnp.maximum(top, jnp.where(slot < live, scores[slot], -1e30))
            top = jnp.max(top, axis=1, keepdims=True) * EXPONENT_SCALE
            total = jnp.zeros((TILE, TILE), F32)
            result = jnp.zeros((TILE, 128), F32)
            for slot in range(KEEP):
                shift = top if slot == 0 else jnp.where(slot < live, top, 1e30)
                exponent = jnp.exp2(scores[slot] * EXPONENT_SCALE - shift)
                total = total + exponent
                result = result + jnp.dot(
                    exponent.astype(BF16), tile_v[head, picks[slot]], preferred_element_type=F32
                )
            total = jnp.sum(total, axis=1, keepdims=True)
            latent = latent + result * (1.0 / total)
        for half in range(2):
            base = half * 128
            packed[side, half] = jnp.where(
                packed_lane < 64, latent[base : base + 64], latent[base + 64 : base + 128]
            )

    def part_targets(owner):
        block = 2 * owner + core
        last = block // 7
        start = 1 - (block + 6) // 7
        own = part_sum.at[owner]
        return (
            (own, block, 32, 128, 0),
            (own.at[pl.ds(96, 32)], block + 1 - last, 160 * last, 32, 1 + last),
            (own.at[pl.ds(0, 32)], block - 1 + start, 160 * (1 - start), 32, 2 - start),
        )

    def to_sibling_part(owner):
        return remote(
            part_out.at[owner, 1 - core],
            sib_in.at[owner],
            sib_send.at[owner],
            sib_recv.at[owner],
            sp=sibling,
        )

    def one_chip(owner):
        place(got_q, 2 * owner, tile_q, 0)
        place(got_q, 2 * owner + 1, tile_q, 0)
        one_tile(owner, 0)
        one_tile(owner, 1)
        for half in range(2):
            pieces = []
            for row in range(4):
                for frame in range(2):
                    for side in range(2):
                        at = (frame * 4 + row) * 8
                        pieces.append(packed[side, half, at : at + 8])
            part_out[owner, half] = jnp.concatenate(pieces, axis=0).astype(BF16)
        exchange_parts = to_sibling_part(owner)
        exchange_parts.start()
        exchange_parts.wait_recv()
        part_sum[owner] = (
            part_out[owner, core].astype(F32) + sib_in[owner].astype(F32)
        ).astype(BF16)
        for kind, (source, target, at, size, region) in enumerate(part_targets(owner)):
            place_at = part_in.at[chip, pl.ds(pl.multiple_of(at, 32), size)]
            arrived = part_recv.at[chip, region]

            @pl.when(target != me)
            def _():
                remote(source, place_at, part_send.at[owner, kind], arrived, sp=target).start()

            @pl.when(target == me)
            def _():
                pltpu.make_async_copy(source, place_at, arrived).start()

    all_lanes = weights_out.at[:, :, lanes]
    to_sibling = remote(all_lanes, all_lanes, w_send.at[11], w_recv.at[11], sp=sibling)

    def chip_turn(turn, carry):
        owner = (
            (turn == 0) * chip + (turn == 1) * near + (turn == 2) * far + (turn == 3) * mirror
        )

        @pl.when(turn == 2)
        def _():
            for copy in x_sends:
                copy.wait()
            to_sibling.start()

        @pl.when(turn > 0)
        def _():
            for k in range(2):
                wait_block(2, got_q, owner * 2 + k)

        one_chip(owner)
        return carry

    wait_block(2, got_q, sibling)
    lax.fori_loop(0, 4, chip_turn, 0)

    latent = jnp.zeros((192, 128), F32)
    for src in range(4):
        for region, (at, size) in enumerate(((32, 128), (0, 32), (160, 32))):
            rows = part_in.at[src, pl.ds(at, size)]
            pltpu.make_async_copy(rows, rows, part_recv.at[src, region]).wait()
        latent = latent + part_in[src].astype(F32)
    seg_latent[seg] = latent.astype(BF16)
    seg_copies = []
    for i, peer in enumerate(x_peers):
        copy = remote(
            seg_latent.at[seg], seg_latent.at[seg], seg_send.at[i], seg_recv.at[i], segment=peer
        )
        copy.start()
        seg_copies.append(copy)
    for copy in seg_copies:
        copy.wait()
    source = jnp.int32(0)
    for micro in range(1, 4):
        source = jnp.where(decode_slot[micro] == seg, micro, source)
    latent_out[...] = seg_latent[source]

    def drain(owner, carry):
        to_sibling_part(owner).wait_send()
        for kind, (source, target, at, size, region) in enumerate(part_targets(owner)):

            @pl.when(target != me)
            def _():
                remote(
                    source,
                    part_in.at[chip, pl.ds(0, size)],
                    part_send.at[owner, kind],
                    part_recv.at[chip, region],
                    sp=target,
                ).wait_send()

        return carry

    lax.fori_loop(0, 4, drain, 0)
    to_sibling.wait()
    for copy in sends:
        copy.wait_send()


def exchange(kept, counts, decode_slot, queries, keys, values, patch, piece):
    any_space = pl.BlockSpec(memory_space=pl.ANY)
    smem = pl.BlockSpec(memory_space=pltpu.SMEM)
    vmem = pl.BlockSpec(memory_space=pltpu.VMEM)
    return pl.pallas_call(
        exchange_kernel,
        out_shape=(
            jax.ShapeDtypeStruct((192, 128), BF16),
            jax.ShapeDtypeStruct((28, CH, CH), BF16),
        ),
        in_specs=[smem, smem, smem] + [any_space] * 5,
        out_specs=(vmem, any_space),
        scratch_shapes=[
            pltpu.VMEM((8, 256, 256), BF16),
            pltpu.VMEM((8, 256, 256), BF16),
            pltpu.VMEM((8, 256, 128), BF16),
            pltpu.VMEM((2, 2, TILE, HD), BF16),
            pltpu.VMEM((2, NT, TILE, HD), BF16),
            pltpu.VMEM((2, NT, TILE, 128), BF16),
            pltpu.VMEM((256, 256), BF16),
            pltpu.VMEM((64, HEADS * HD), BF16),
            pltpu.VMEM((256, HEADS * HD), BF16),
            pltpu.VMEM((8, 256, 128), BF16),
            pltpu.VMEM((2, 2, 64, 128), F32),
            pltpu.VMEM((4, 2, 128, 128), BF16),
            pltpu.VMEM((4, 128, 128), BF16),
            pltpu.VMEM((4, 128, 128), BF16),
            pltpu.VMEM((4, 192, 128), BF16),
            pltpu.VMEM((4, 192, 128), BF16),
            pltpu.SemaphoreType.DMA((3, 7)),
            pltpu.SemaphoreType.DMA((3, 8)),
            pltpu.SemaphoreType.DMA((4,)),
            pltpu.SemaphoreType.DMA((4,)),
            pltpu.SemaphoreType.DMA((4,)),
            pltpu.SemaphoreType.DMA((4, 3)),
            pltpu.SemaphoreType.DMA((4, 3)),
            pltpu.SemaphoreType.DMA((3,)),
            pltpu.SemaphoreType.DMA((3,)),
            pltpu.SemaphoreType.DMA,
            pltpu.SemaphoreType.DMA((12,)),
            pltpu.SemaphoreType.DMA((12,)),
        ],
        compiler_params=pltpu.CompilerParams(
            collective_id=0, has_side_effects=True, vmem_limit_bytes=60 << 20
        ),
        cost_estimate=pl.CostEstimate(
            flops=4 * 16 * 4 * 256 * 256 * 128, bytes_accessed=10 << 20, transcendentals=1 << 22
        ),
    )(kept, counts, decode_slot, queries, keys, values, patch, piece)


def slot_of(offset):
    return offset if offset < 21 else offset + 1


def decode_kernel(
    latent, first_kernel, weights, out, window, first, act, weights_vmem, weight_sem
):
    me = lax.axis_index("sp")
    load = pltpu.make_async_copy(weights, weights_vmem, weight_sem)
    load.start()

    twice = (
        lax.broadcasted_iota(jnp.int32, (384, 192), 0) // 2
        == lax.broadcasted_iota(jnp.int32, (384, 192), 1)
    ).astype(BF16)
    doubled = jnp.dot(twice, latent[...], preferred_element_type=F32)
    column = lax.broadcasted_iota(jnp.int32, (384, 128), 0) % 32
    here = jnp.where(column % 2 == 0, doubled, pltpu.roll(doubled, 128 - LAT, axis=1))
    before = jnp.where(column == 0, here, pltpu.roll(here, 1, axis=0))
    after = jnp.where(column == 31, here, pltpu.roll(here, 383, axis=0))
    source_lane = lax.broadcasted_iota(jnp.int32, (384, 512), 0)
    target_lane = lax.broadcasted_iota(jnp.int32, (384, 512), 1)
    slot = target_lane % 128
    wanted = (slot // LAT) * 128 + (target_lane // 128) * 32 + slot % LAT
    pick = jnp.logical_and(slot < 48, source_lane == wanted).astype(BF16)
    joined = jnp.dot(
        jnp.concatenate([before, here, after], axis=1).astype(BF16),
        pick,
        preferred_element_type=F32,
    ).astype(BF16)
    for row in range(6):
        for frame_low in range(2):
            at = (row * 2 + frame_low) * 32
            for frame_high in range(2):
                for up in range(2):
                    lane = (frame_high * 2 + up) * 128
                    window[frame_high * 2 + frame_low, 2 * row + up] = joined[
                        at : at + 32, lane : lane + 128
                    ]

    @pl.when(me == 0)
    def _():
        window[:, 1] = window[:, 2]

    @pl.when(me == 7)
    def _():
        window[:, 10] = window[:, 9]

    wide_column = lax.broadcasted_iota(jnp.int32, (320, CH), 0) % 32
    for frame in range(4):
        total = jnp.zeros((320, CH), F32)
        for time in range(3):
            source = max(frame + time - 2, 0)
            for row in range(3):
                offset = (time * 3 + row) * 48
                total = total + jnp.dot(
                    window[source, row : row + 10, :, 0:48].reshape(320, 48),
                    first_kernel[offset : offset + 48],
                    preferred_element_type=F32,
                )
        rounded = (total * VAE_SCALE).astype(BF16)
        first[frame * 256 : frame * 256 + 256] = rounded[32:288]
        wide = rounded.astype(F32)
        wide = (wide / (1.0 + jnp.exp(-wide))).astype(BF16).astype(F32)
        before = jnp.where(wide_column == 0, wide, pltpu.roll(wide, 1, axis=0))
        after = jnp.where(wide_column == 31, wide, pltpu.roll(wide, 319, axis=0))
        for place, part in enumerate((before, wide, after)):
            part = part.reshape(10, 32, CH).astype(BF16)
            act[frame + 2, :, :, place * CH : place * CH + CH] = part
            if frame == 0:
                act[0, :, :, place * CH : place * CH + CH] = part
                act[1, :, :, place * CH : place * CH + CH] = part

    @pl.when(me == 0)
    def _():
        act[:, 0] = act[:, 1]

    @pl.when(me == 7)
    def _():
        act[:, 9] = act[:, 8]

    load.wait()
    for part in range(2):
        total = first[part * 512 : part * 512 + 512].astype(F32)
        for time in range(3):
            for row in range(3):
                slot = slot_of((time * 3 + row) * 3)
                block = act[part * 2 + time : part * 2 + time + 2, row : row + 8]
                total = total + jnp.dot(
                    block.reshape(512, 3 * CH),
                    weights_vmem[slot : slot + 3].reshape(3 * CH, CH),
                    preferred_element_type=F32,
                )
        out[part * 512 : part * 512 + 512] = total.astype(BF16)


def decode(latent, first_kernel, weights):
    vmem = pl.BlockSpec(memory_space=pltpu.VMEM)
    return pl.pallas_call(
        decode_kernel,
        out_shape=jax.ShapeDtypeStruct((1024, CH), BF16),
        in_specs=[vmem, vmem, pl.BlockSpec(memory_space=pl.ANY)],
        out_specs=vmem,
        scratch_shapes=[
            pltpu.VMEM((4, 12, 32, 128), BF16),
            pltpu.VMEM((1024, CH), BF16),
            pltpu.VMEM((6, 10, 32, 3 * CH), BF16),
            pltpu.VMEM((28, CH, CH), BF16),
            pltpu.SemaphoreType.DMA,
        ],
        compiler_params=pltpu.CompilerParams(vmem_limit_bytes=60 << 20),
        cost_estimate=pl.CostEstimate(
            flops=2 * 1024 * 27 * 256 * 256, bytes_accessed=5 << 20, transcendentals=1 << 19
        ),
    )(latent, first_kernel, weights)


def local(
    queries,
    key_states,
    value_states,
    kept_tiles,
    kept_counts,
    patch_weight,
    decode_slot,
    first_kernel,
    second_kernel,
):
    latent, weights = exchange(
        kept_tiles.transpose(1, 2, 0),
        kept_counts.transpose(1, 0),
        decode_slot,
        queries.reshape(256, HEADS * HD),
        key_states.reshape(256, HEADS * HD),
        value_states.reshape(256, HEADS * HD),
        patch_weight.transpose(1, 0),
        second_kernel,
    )
    decoded = decode(latent, first_kernel.reshape(27 * LAT, CH), weights)
    return decoded.reshape(1, 1, 4, 8, 32, CH)


def solution(mesh):
    tokens = P("segment", "grp", None, "sp", None, None)
    return jax.shard_map(
        local,
        mesh=mesh,
        in_specs=(tokens, tokens, tokens, P(), P(), P(), P(), P(), P(None, "grp", None)),
        out_specs=tokens,
        check_vma=False,
    )
```

```python
import functools
import math

import jax
import jax.numpy as jnp
from jax import lax
from jax.experimental import pallas as pl
from jax.experimental.pallas import tpu as pltpu
from jax.sharding import PartitionSpec as P

HEADS = 16
HD = 128
LAT = 16
CH = 256
NT = 8
KEEP = 4
TILE = 256
VAE_SCALE = 1.0 / 0.476986
MESH = pl.DeviceIdType.MESH
BF16 = jnp.bfloat16
F32 = jnp.float32
EXPONENT_SCALE = HD**-0.5 * math.log2(math.e)


def remote(src, dst, send_sem, recv_sem, **where):
    return pltpu.make_async_remote_copy(
        src_ref=src,
        dst_ref=dst,
        send_sem=send_sem,
        recv_sem=recv_sem,
        device_id=where,
        device_id_type=MESH,
    )


def exchange_kernel(
    kept,
    counts,
    decode_slot,
    queries,
    keys,
    values,
    patch,
    piece,
    latent_out,
    weights_out,
    got_q,
    got_k,
    got_v,
    tile_q,
    tile_k,
    tile_v,
    order,
    patch_all,
    own_values,
    projected,
    packed,
    part_out,
    sib_in,
    part_sum,
    part_in,
    seg_latent,
    send_sem,
    recv_sem,
    local_sem,
    sib_send,
    sib_recv,
    part_send,
    part_recv,
    seg_send,
    seg_recv,
    w_local,
    w_send,
    w_recv,
):
    me = lax.axis_index("sp")
    seg = lax.axis_index("segment")
    grp = lax.axis_index("grp")
    chip = me // 2
    core = me % 2
    sibling = chip * 2 + 1 - core
    far = (chip + 2) % 4
    mirror = 3 - chip
    near = chip + 1 - 2 * (chip % 2)
    peers = [
        far * 2 + core,
        far * 2 + 1 - core,
        mirror * 2 + core,
        mirror * 2 + 1 - core,
        near * 2 + core,
        near * 2 + 1 - core,
        sibling,
    ]
    z_partner = grp + 1 - 2 * (grp % 2)
    y_peers = [(grp + 2 * step) % 16 for step in range(1, 8)]
    x_peers = [(seg + step) % 4 for step in range(1, 4)]

    barrier = pltpu.get_barrier_semaphore()
    for peer in peers:
        pl.semaphore_signal(barrier, inc=1, device_id={"sp": peer}, device_id_type=MESH)
    for peer in x_peers:
        pl.semaphore_signal(barrier, inc=1, device_id={"segment": peer}, device_id_type=MESH)
    for peer in [z_partner] + y_peers:
        pl.semaphore_signal(barrier, inc=1, device_id={"grp": peer}, device_id_type=MESH)
    pl.semaphore_wait(barrier, 18)

    sends = []

    def send(a, source, target):
        for i, peer in enumerate(peers):
            copy = remote(source(peer), target.at[me], send_sem.at[a, i], recv_sem.at[a, me], sp=peer)
            copy.start()
            sends.append(copy)

    def columns_of(ref):
        return lambda peer: ref.at[:, pl.ds(pl.multiple_of(peer * 256, 256), 256)]

    load_values = pltpu.make_async_copy(values, own_values, local_sem.at[0])
    load_values.start()
    load_patch = pltpu.make_async_copy(patch, patch_all, local_sem.at[1])
    load_patch.start()
    send(0, columns_of(keys), got_k)
    keep_keys = pltpu.make_async_copy(columns_of(keys)(me), got_k.at[me], local_sem.at[2])
    keep_keys.start()
    keep_queries = pltpu.make_async_copy(columns_of(queries)(me), got_q.at[me], local_sem.at[3])
    keep_queries.start()

    quarter = seg * 7
    taps = pl.ds(quarter, 7)
    lanes = pl.ds(pl.multiple_of(core * 128, 128), 128)
    own_part = piece.at[pl.ds(quarter - seg // 3, 7), :, lanes]
    own_rows = pl.ds(pl.multiple_of(grp * 16, 16), 16)
    w_keep = pltpu.make_async_copy(own_part, weights_out.at[taps, own_rows, lanes], w_local)
    w_keep.start()
    w_cross = remote(
        own_part, weights_out.at[taps, own_rows, lanes], w_send.at[0], w_recv.at[0], grp=z_partner
    )
    w_cross.start()

    load_values.wait()
    load_patch.wait()
    patch_lane = lax.broadcasted_iota(jnp.int32, (64, 256), 1)

    def project(peer, carry):
        columns = pl.ds(pl.multiple_of(peer * 256, 256), 256)
        weight = patch_all[:, columns].astype(F32)
        weight = jnp.concatenate(
            [jnp.where(patch_lane < HD, weight, 0.0), jnp.where(patch_lane < HD, 0.0, weight)],
            axis=0,
        ).astype(BF16)
        projected[peer] = lax.dot_general(
            own_values[:, columns],
            weight,
            (((1,), (1,)), ((), ())),
            preferred_element_type=F32,
        ).astype(BF16)
        return carry

    lax.fori_loop(0, 8, project, 0)
    send(1, lambda peer: projected.at[peer], got_v)
    got_v[me] = projected[me]
    send(2, columns_of(queries), got_q)

    w_keep.wait()
    w_cross.wait()
    pair_rows = pl.ds(pl.multiple_of((grp // 2) * 32, 32), 32)
    y_sends = []
    for i, peer in enumerate(y_peers):
        block = weights_out.at[taps, pair_rows, lanes]
        copy = remote(block, block, w_send.at[1 + i], w_recv.at[1 + i], grp=peer)
        copy.start()
        y_sends.append(copy)
    keep_keys.wait()
    keep_queries.wait()
    def wait_block(a, target, src):
        remote(
            target.at[src], target.at[src], send_sem.at[a, 0], recv_sem.at[a, src], sp=sibling
        ).wait_recv()

    to_row = lax.broadcasted_iota(jnp.int32, (256, 256), 0)
    from_row = lax.broadcasted_iota(jnp.int32, (256, 256), 1)
    wanted = ((to_row % 128) // 8) * 16 + (to_row // 128) * 8 + to_row % 8
    order[...] = (from_row == wanted).astype(BF16)

    def place(got, src, tiles, first_tile):
        block = jnp.dot(order[...], got[src], preferred_element_type=F32).astype(BF16)
        rows = pl.ds(pl.multiple_of((src % 2) * 128, 128), 128)
        for head in range(2):
            for side in range(2):
                tiles[head, first_tile + side, rows] = block[
                    side * 128 : side * 128 + 128, head * 128 : head * 128 + 128
                ]

    value_lane = lax.broadcasted_iota(jnp.int32, (256, 128), 1)

    def place_keys(src):
        place(got_k, src, tile_k, 2 * (src // 2))
        block = jnp.dot(order[...], got_v[src], preferred_element_type=F32)
        turned = pltpu.roll(block, 64, axis=1)
        rows = pl.ds(pl.multiple_of((src % 2) * 128, 128), 128)
        for head, (left, right) in enumerate(((block, turned), (turned, block))):
            both = jnp.where(value_lane < 64, left, right).astype(BF16)
            for side in range(2):
                tile_v[head, 2 * (src // 2) + side, rows] = both[side * 128 : side * 128 + 128]

    place_keys(me)
    for peer in (peers[6], peers[4], peers[5]):
        wait_block(0, got_k, peer)
        wait_block(1, got_v, peer)
        place_keys(peer)

    for copy in y_sends:
        copy.wait()
    x_sends = []
    own_quarter = weights_out.at[taps, :, lanes]
    for i, peer in enumerate(x_peers):
        copy = remote(own_quarter, own_quarter, w_send.at[8 + i], w_recv.at[8 + i], segment=peer)
        copy.start()
        x_sends.append(copy)

    for peer in peers[:4]:
        wait_block(0, got_k, peer)
        wait_block(1, got_v, peer)
        place_keys(peer)

    head_base = me * 2
    packed_lane = lax.broadcasted_iota(jnp.int32, (64, 128), 1)

    def one_tile(owner, side):
        tile = 2 * owner + side
        latent = jnp.zeros((TILE, 128), F32)
        for head in range(2):
            query = tile_q[head, side]
            live = counts[tile, head_base + head]
            scores, picks = [], []
            for slot in range(KEEP):
                pick = kept[tile, slot, head_base + head]
                picks.append(pick)
                scores.append(
                    lax.dot_general(
                        query,
                        tile_k[head, pick],
                        (((1,), (1,)), ((), ())),
                        preferred_element_type=F32,
                    )
                )
            top = scores[0]
            for slot in range(1, KEEP):
                top = jnp.maximum(top, jnp.where(slot < live, scores[slot], -1e30))
            top = jnp.max(top, axis=1, keepdims=True) * EXPONENT_SCALE
            total = jnp.zeros((TILE, TILE), F32)
            result = jnp.zeros((TILE, 128), F32)
            for slot in range(KEEP):
                shift = top if slot == 0 else jnp.where(slot < live, top, 1e30)
                exponent = jnp.exp2(scores[slot] * EXPONENT_SCALE - shift)
                total = total + exponent
                result = result + jnp.dot(
                    exponent.astype(BF16), tile_v[head, picks[slot]], preferred_element_type=F32
                )
            total = jnp.sum(total, axis=1, keepdims=True)
            latent = latent + result * (1.0 / total)
        for half in range(2):
            base = half * 128
            packed[side, half] = jnp.where(
                packed_lane < 64, latent[base : base + 64], latent[base + 64 : base + 128]
            )

    def part_targets(owner):
        block = 2 * owner + core
        last = block // 7
        start = 1 - (block + 6) // 7
        own = part_sum.at[owner]
        return (
            (own, block, 32, 128, 0),
            (own.at[pl.ds(96, 32)], block + 1 - last, 160 * last, 32, 1 + last),
            (own.at[pl.ds(0, 32)], block - 1 + start, 160 * (1 - start), 32, 2 - start),
        )

    def to_sibling_part(owner):
        return remote(
            part_out.at[owner, 1 - core],
            sib_in.at[owner],
            sib_send.at[owner],
            sib_recv.at[owner],
            sp=sibling,
        )

    def one_chip(owner):
        place(got_q, 2 * owner, tile_q, 0)
        place(got_q, 2 * owner + 1, tile_q, 0)
        one_tile(owner, 0)
        one_tile(owner, 1)
        for half in range(2):
            pieces = []
            for row in range(4):
                for frame in range(2):
                    for side in range(2):
                        at = (frame * 4 + row) * 8
                        pieces.append(packed[side, half, at : at + 8])
            part_out[owner, half] = jnp.concatenate(pieces, axis=0).astype(BF16)
        exchange_parts = to_sibling_part(owner)
        exchange_parts.start()
        exchange_parts.wait_recv()
        part_sum[owner] = (
            part_out[owner, core].astype(F32) + sib_in[owner].astype(F32)
        ).astype(BF16)
        for kind, (source, target, at, size, region) in enumerate(part_targets(owner)):
            place_at = part_in.at[chip, pl.ds(pl.multiple_of(at, 32), size)]
            arrived = part_recv.at[chip, region]

            @pl.when(target != me)
            def _():
                remote(source, place_at, part_send.at[owner, kind], arrived, sp=target).start()

            @pl.when(target == me)
            def _():
                pltpu.make_async_copy(source, place_at, arrived).start()

    all_lanes = weights_out.at[:, :, lanes]
    to_sibling = remote(all_lanes, all_lanes, w_send.at[11], w_recv.at[11], sp=sibling)

    def chip_turn(turn, carry):
        owner = (
            (turn == 0) * chip + (turn == 1) * near + (turn == 2) * far + (turn == 3) * mirror
        )

        @pl.when(turn > 0)
        def _():
            for k in range(2):
                wait_block(2, got_q, owner * 2 + k)

        one_chip(owner)
        return carry

    wait_block(2, got_q, sibling)
    lax.fori_loop(0, 4, chip_turn, 0)
    for copy in x_sends:
        copy.wait()
    to_sibling.start()

    latent = jnp.zeros((192, 128), F32)
    for src in range(4):
        for region, (at, size) in enumerate(((32, 128), (0, 32), (160, 32))):
            rows = part_in.at[src, pl.ds(at, size)]
            pltpu.make_async_copy(rows, rows, part_recv.at[src, region]).wait()
        latent = latent + part_in[src].astype(F32)
    seg_latent[seg] = latent.astype(BF16)
    seg_copies = []
    for i, peer in enumerate(x_peers):
        copy = remote(
            seg_latent.at[seg], seg_latent.at[seg], seg_send.at[i], seg_recv.at[i], segment=peer
        )
        copy.start()
        seg_copies.append(copy)
    for copy in seg_copies:
        copy.wait()
    source = jnp.int32(0)
    for micro in range(1, 4):
        source = jnp.where(decode_slot[micro] == seg, micro, source)
    latent_out[...] = seg_latent[source]

    def drain(owner, carry):
        to_sibling_part(owner).wait_send()
        for kind, (source, target, at, size, region) in enumerate(part_targets(owner)):

            @pl.when(target != me)
            def _():
                remote(
                    source,
                    part_in.at[chip, pl.ds(0, size)],
                    part_send.at[owner, kind],
                    part_recv.at[chip, region],
                    sp=target,
                ).wait_send()

        return carry

    lax.fori_loop(0, 4, drain, 0)
    to_sibling.wait()
    for copy in sends:
        copy.wait_send()


def exchange(kept, counts, decode_slot, queries, keys, values, patch, piece):
    any_space = pl.BlockSpec(memory_space=pl.ANY)
    smem = pl.BlockSpec(memory_space=pltpu.SMEM)
    vmem = pl.BlockSpec(memory_space=pltpu.VMEM)
    return pl.pallas_call(
        exchange_kernel,
        out_shape=(
            jax.ShapeDtypeStruct((192, 128), BF16),
            jax.ShapeDtypeStruct((28, CH, CH), BF16),
        ),
        in_specs=[smem, smem, smem] + [any_space] * 5,
        out_specs=(vmem, any_space),
        scratch_shapes=[
            pltpu.VMEM((8, 256, 256), BF16),
            pltpu.VMEM((8, 256, 256), BF16),
            pltpu.VMEM((8, 256, 128), BF16),
            pltpu.VMEM((2, 2, TILE, HD), BF16),
            pltpu.VMEM((2, NT, TILE, HD), BF16),
            pltpu.VMEM((2, NT, TILE, 128), BF16),
            pltpu.VMEM((256, 256), BF16),
            pltpu.VMEM((64, HEADS * HD), BF16),
            pltpu.VMEM((256, HEADS * HD), BF16),
            pltpu.VMEM((8, 256, 128), BF16),
            pltpu.VMEM((2, 2, 64, 128), F32),
            pltpu.VMEM((4, 2, 128, 128), BF16),
            pltpu.VMEM((4, 128, 128), BF16),
            pltpu.VMEM((4, 128, 128), BF16),
            pltpu.VMEM((4, 192, 128), BF16),
            pltpu.VMEM((4, 192, 128), BF16),
            pltpu.SemaphoreType.DMA((3, 7)),
            pltpu.SemaphoreType.DMA((3, 8)),
            pltpu.SemaphoreType.DMA((4,)),
            pltpu.SemaphoreType.DMA((4,)),
            pltpu.SemaphoreType.DMA((4,)),
            pltpu.SemaphoreType.DMA((4, 3)),
            pltpu.SemaphoreType.DMA((4, 3)),
            pltpu.SemaphoreType.DMA((3,)),
            pltpu.SemaphoreType.DMA((3,)),
            pltpu.SemaphoreType.DMA,
            pltpu.SemaphoreType.DMA((12,)),
            pltpu.SemaphoreType.DMA((12,)),
        ],
        compiler_params=pltpu.CompilerParams(
            collective_id=0, has_side_effects=True, vmem_limit_bytes=60 << 20
        ),
        cost_estimate=pl.CostEstimate(
            flops=4 * 16 * 4 * 256 * 256 * 128, bytes_accessed=10 << 20, transcendentals=1 << 22
        ),
    )(kept, counts, decode_slot, queries, keys, values, patch, piece)


def slot_of(offset):
    return offset if offset < 21 else offset + 1


def decode_kernel(
    latent, first_kernel, weights, out, window, rows, first, act, weights_vmem, weight_sem
):
    me = lax.axis_index("sp")
    load = pltpu.make_async_copy(weights, weights_vmem, weight_sem)
    load.start()

    twice = (
        lax.broadcasted_iota(jnp.int32, (384, 192), 0) // 2
        == lax.broadcasted_iota(jnp.int32, (384, 192), 1)
    ).astype(BF16)
    doubled = jnp.dot(twice, latent[...], preferred_element_type=F32)
    column = lax.broadcasted_iota(jnp.int32, (384, 128), 0) % 32
    here = jnp.where(column % 2 == 0, doubled, pltpu.roll(doubled, 128 - LAT, axis=1))
    before = jnp.where(column == 0, here, pltpu.roll(here, 1, axis=0))
    after = jnp.where(column == 31, here, pltpu.roll(here, 383, axis=0))
    source_lane = lax.broadcasted_iota(jnp.int32, (384, 512), 0)
    target_lane = lax.broadcasted_iota(jnp.int32, (384, 512), 1)
    slot = target_lane % 128
    wanted = (slot // LAT) * 128 + (target_lane // 128) * 32 + slot % LAT
    pick = jnp.logical_and(slot < 48, source_lane == wanted).astype(BF16)
    joined = jnp.dot(
        jnp.concatenate([before, here, after], axis=1).astype(BF16),
        pick,
        preferred_element_type=F32,
    ).astype(BF16)
    for row in range(6):
        for frame_low in range(2):
            at = (row * 2 + frame_low) * 32
            for frame_high in range(2):
                for up in range(2):
                    lane = (frame_high * 2 + up) * 128
                    window[frame_high * 2 + frame_low, 2 * row + up] = joined[
                        at : at + 32, lane : lane + 128
                    ]

    @pl.when(me == 0)
    def _():
        window[:, 1] = window[:, 2]

    @pl.when(me == 7)
    def _():
        window[:, 10] = window[:, 9]

    for frame in range(4):
        rows[frame] = jnp.concatenate(
            [window[frame, row : row + 10, :, 0:48].reshape(320, 48) for row in range(3)], axis=1
        )
    wide_column = lax.broadcasted_iota(jnp.int32, (320, CH), 0) % 32
    for frame in range(4):
        total = jnp.zeros((320, CH), F32)
        for time in range(3):
            total = total + jnp.dot(
                rows[max(frame + time - 2, 0)],
                first_kernel[time * 144 : time * 144 + 144],
                preferred_element_type=F32,
            )
        rounded = (total * VAE_SCALE).astype(BF16)
        first[frame * 256 : frame * 256 + 256] = rounded[32:288]
        wide = rounded.astype(F32)
        wide = (wide / (1.0 + jnp.exp(-wide))).astype(BF16).astype(F32)
        before = jnp.where(wide_column == 0, wide, pltpu.roll(wide, 1, axis=0))
        after = jnp.where(wide_column == 31, wide, pltpu.roll(wide, 319, axis=0))
        for place, part in enumerate((before, wide, after)):
            part = part.reshape(10, 32, CH).astype(BF16)
            act[frame + 2, :, :, place * CH : place * CH + CH] = part
            if frame == 0:
                act[0, :, :, place * CH : place * CH + CH] = part
                act[1, :, :, place * CH : place * CH + CH] = part

    @pl.when(me == 0)
    def _():
        act[:, 0] = act[:, 1]

    @pl.when(me == 7)
    def _():
        act[:, 9] = act[:, 8]

    load.wait()
    for part in range(2):
        total = first[part * 512 : part * 512 + 512].astype(F32)
        for time in range(3):
            for row in range(3):
                slot = slot_of((time * 3 + row) * 3)
                block = act[part * 2 + time : part * 2 + time + 2, row : row + 8]
                total = total + jnp.dot(
                    block.reshape(512, 3 * CH),
                    weights_vmem[slot : slot + 3].reshape(3 * CH, CH),
                    preferred_element_type=F32,
                )
        out[part * 512 : part * 512 + 512] = total.astype(BF16)


def decode(latent, first_kernel, weights):
    vmem = pl.BlockSpec(memory_space=pltpu.VMEM)
    return pl.pallas_call(
        decode_kernel,
        out_shape=jax.ShapeDtypeStruct((1024, CH), BF16),
        in_specs=[vmem, vmem, pl.BlockSpec(memory_space=pl.ANY)],
        out_specs=vmem,
        scratch_shapes=[
            pltpu.VMEM((4, 12, 32, 128), BF16),
            pltpu.VMEM((4, 320, 144), BF16),
            pltpu.VMEM((1024, CH), BF16),
            pltpu.VMEM((6, 10, 32, 3 * CH), BF16),
            pltpu.VMEM((28, CH, CH), BF16),
            pltpu.SemaphoreType.DMA,
        ],
        compiler_params=pltpu.CompilerParams(vmem_limit_bytes=60 << 20),
        cost_estimate=pl.CostEstimate(
            flops=2 * 1024 * 27 * 256 * 256, bytes_accessed=5 << 20, transcendentals=1 << 19
        ),
    )(latent, first_kernel, weights)


def local(
    queries,
    key_states,
    value_states,
    kept_tiles,
    kept_counts,
    patch_weight,
    decode_slot,
    first_kernel,
    second_kernel,
):
    latent, weights = exchange(
        kept_tiles.transpose(1, 2, 0),
        kept_counts.transpose(1, 0),
        decode_slot,
        queries.reshape(256, HEADS * HD),
        key_states.reshape(256, HEADS * HD),
        value_states.reshape(256, HEADS * HD),
        patch_weight.transpose(1, 0),
        second_kernel,
    )
    decoded = decode(latent, first_kernel.reshape(27 * LAT, CH), weights)
    return decoded.reshape(1, 1, 4, 8, 32, CH)


def solution(mesh):
    tokens = P("segment", "grp", None, "sp", None, None)
    return jax.shard_map(
        local,
        mesh=mesh,
        in_specs=(tokens, tokens, tokens, P(), P(), P(), P(), P(), P(None, "grp", None)),
        out_specs=tokens,
        check_vma=False,
    )
```

```python
import functools
import math

import jax
import jax.numpy as jnp
from jax import lax
from jax.experimental import pallas as pl
from jax.experimental.pallas import tpu as pltpu
from jax.sharding import PartitionSpec as P

HEADS = 16
HD = 128
LAT = 16
CH = 256
NT = 8
KEEP = 4
TILE = 256
VAE_SCALE = 1.0 / 0.476986
MESH = pl.DeviceIdType.MESH
BF16 = jnp.bfloat16
F32 = jnp.float32
EXPONENT_SCALE = HD**-0.5 * math.log2(math.e)


def remote(src, dst, send_sem, recv_sem, **where):
    return pltpu.make_async_remote_copy(
        src_ref=src,
        dst_ref=dst,
        send_sem=send_sem,
        recv_sem=recv_sem,
        device_id=where,
        device_id_type=MESH,
    )


def exchange_kernel(
    kept,
    counts,
    decode_slot,
    queries,
    keys,
    values,
    patch,
    piece,
    latent_out,
    weights_out,
    got_q,
    got_k,
    got_v,
    tile_q,
    tile_k,
    tile_v,
    order,
    patch_all,
    own_values,
    projected,
    packed,
    part_out,
    sib_in,
    part_sum,
    part_in,
    seg_latent,
    send_sem,
    recv_sem,
    local_sem,
    sib_send,
    sib_recv,
    part_send,
    part_recv,
    seg_send,
    seg_recv,
    w_local,
    w_send,
    w_recv,
):
    me = lax.axis_index("sp")
    seg = lax.axis_index("segment")
    grp = lax.axis_index("grp")
    chip = me // 2
    core = me % 2
    sibling = chip * 2 + 1 - core
    far = (chip + 2) % 4
    mirror = 3 - chip
    near = chip + 1 - 2 * (chip % 2)
    peers = [
        far * 2 + core,
        far * 2 + 1 - core,
        mirror * 2 + core,
        mirror * 2 + 1 - core,
        near * 2 + core,
        near * 2 + 1 - core,
        sibling,
    ]
    z_partner = grp + 1 - 2 * (grp % 2)
    y_peers = [(grp + 2 * step) % 16 for step in range(1, 8)]
    x_peers = [(seg + step) % 4 for step in range(1, 4)]

    barrier = pltpu.get_barrier_semaphore()
    for peer in peers:
        pl.semaphore_signal(barrier, inc=1, device_id={"sp": peer}, device_id_type=MESH)
    for peer in x_peers:
        pl.semaphore_signal(barrier, inc=1, device_id={"segment": peer}, device_id_type=MESH)
    for peer in y_peers:
        pl.semaphore_signal(barrier, inc=1, device_id={"grp": peer}, device_id_type=MESH)
    at_border = chip % 3 == 0
    source_chip = 3 * (1 - chip // 2)
    pl.semaphore_signal(
        barrier,
        inc=1,
        device_id={"grp": z_partner, "sp": source_chip * 2 + core},
        device_id_type=MESH,
    )
    pl.semaphore_wait(barrier, 17 + 2 * at_border.astype(jnp.int32))

    quarter = seg * 7
    taps = pl.ds(quarter, 7)
    lanes = pl.ds(pl.multiple_of(core * 128, 128), 128)
    own_part = piece.at[pl.ds(quarter - seg // 3, 7), :, lanes]
    own_rows = pl.ds(pl.multiple_of(grp * 16, 16), 16)
    own_place = weights_out.at[taps, own_rows, lanes]
    w_keep = pltpu.make_async_copy(own_part, own_place, w_local)
    w_keep.start()
    beyond = mirror + 1 - 2 * (mirror % 2)
    w_cross = [
        remote(
            own_part,
            own_place,
            w_send.at[place],
            w_recv.at[0],
            grp=z_partner,
            sp=target * 2 + core,
        )
        for place, target in ((0, mirror), (12, beyond))
    ]

    @pl.when(at_border)
    def _():
        for copy in w_cross:
            copy.start()

    sends = []

    def send(a, source, target):
        for i, peer in enumerate(peers):
            copy = remote(source(peer), target.at[me], send_sem.at[a, i], recv_sem.at[a, me], sp=peer)
            copy.start()
            sends.append(copy)

    def columns_of(ref):
        return lambda peer: ref.at[:, pl.ds(pl.multiple_of(peer * 256, 256), 256)]

    load_values = pltpu.make_async_copy(values, own_values, local_sem.at[0])
    load_values.start()
    load_patch = pltpu.make_async_copy(patch, patch_all, local_sem.at[1])
    load_patch.start()
    send(0, columns_of(keys), got_k)
    keep_keys = pltpu.make_async_copy(columns_of(keys)(me), got_k.at[me], local_sem.at[2])
    keep_keys.start()
    keep_queries = pltpu.make_async_copy(columns_of(queries)(me), got_q.at[me], local_sem.at[3])
    keep_queries.start()

    load_values.wait()
    load_patch.wait()
    patch_lane = lax.broadcasted_iota(jnp.int32, (64, 256), 1)

    def project(peer, carry):
        columns = pl.ds(pl.multiple_of(peer * 256, 256), 256)
        weight = patch_all[:, columns].astype(F32)
        weight = jnp.concatenate(
            [jnp.where(patch_lane < HD, weight, 0.0), jnp.where(patch_lane < HD, 0.0, weight)],
            axis=0,
        ).astype(BF16)
        projected[peer] = lax.dot_general(
            own_values[:, columns],
            weight,
            (((1,), (1,)), ((), ())),
            preferred_element_type=F32,
        ).astype(BF16)
        return carry

    lax.fori_loop(0, 8, project, 0)
    send(1, lambda peer: projected.at[peer], got_v)
    got_v[me] = projected[me]
    send(2, columns_of(queries), got_q)

    w_keep.wait()
    w_cross[0].wait_recv()

    @pl.when(at_border)
    def _():
        for copy in w_cross:
            copy.wait_send()

    pair_rows = pl.ds(pl.multiple_of((grp // 2) * 32, 32), 32)
    y_sends = []
    for i, peer in enumerate(y_peers):
        block = weights_out.at[taps, pair_rows, lanes]
        copy = remote(block, block, w_send.at[1 + i], w_recv.at[1 + i], grp=peer)
        copy.start()
        y_sends.append(copy)
    keep_keys.wait()
    keep_queries.wait()
    def wait_block(a, target, src):
        remote(
            target.at[src], target.at[src], send_sem.at[a, 0], recv_sem.at[a, src], sp=sibling
        ).wait_recv()

    to_row = lax.broadcasted_iota(jnp.int32, (256, 256), 0)
    from_row = lax.broadcasted_iota(jnp.int32, (256, 256), 1)
    wanted = ((to_row % 128) // 8) * 16 + (to_row // 128) * 8 + to_row % 8
    order[...] = (from_row == wanted).astype(BF16)

    def place(got, src, tiles, first_tile):
        block = jnp.dot(order[...], got[src], preferred_element_type=F32).astype(BF16)
        rows = pl.ds(pl.multiple_of((src % 2) * 128, 128), 128)
        for head in range(2):
            for side in range(2):
                tiles[head, first_tile + side, rows] = block[
                    side * 128 : side * 128 + 128, head * 128 : head * 128 + 128
                ]

    value_lane = lax.broadcasted_iota(jnp.int32, (256, 128), 1)

    def place_keys(src):
        place(got_k, src, tile_k, 2 * (src // 2))
        block = jnp.dot(order[...], got_v[src], preferred_element_type=F32)
        turned = pltpu.roll(block, 64, axis=1)
        rows = pl.ds(pl.multiple_of((src % 2) * 128, 128), 128)
        for head, (left, right) in enumerate(((block, turned), (turned, block))):
            both = jnp.where(value_lane < 64, left, right).astype(BF16)
            for side in range(2):
                tile_v[head, 2 * (src // 2) + side, rows] = both[side * 128 : side * 128 + 128]

    place_keys(me)
    for peer in (peers[6], peers[4], peers[5]):
        wait_block(0, got_k, peer)
        wait_block(1, got_v, peer)
        place_keys(peer)

    for copy in y_sends:
        copy.wait()
    x_sends = []
    own_quarter = weights_out.at[taps, :, lanes]
    for i, peer in enumerate(x_peers):
        copy = remote(own_quarter, own_quarter, w_send.at[8 + i], w_recv.at[8 + i], segment=peer)
        copy.start()
        x_sends.append(copy)

    for peer in peers[:4]:
        wait_block(0, got_k, peer)
        wait_block(1, got_v, peer)
        place_keys(peer)

    head_base = me * 2
    packed_lane = lax.broadcasted_iota(jnp.int32, (64, 128), 1)

    def one_tile(owner, side):
        tile = 2 * owner + side
        latent = jnp.zeros((TILE, 128), F32)
        for head in range(2):
            query = tile_q[head, side]
            live = counts[tile, head_base + head]
            scores, picks = [], []
            for slot in range(KEEP):
                pick = kept[tile, slot, head_base + head]
                picks.append(pick)
                scores.append(
                    lax.dot_general(
                        query,
                        tile_k[head, pick],
                        (((1,), (1,)), ((), ())),
                        preferred_element_type=F32,
                    )
                )
            top = scores[0]
            for slot in range(1, KEEP):
                top = jnp.maximum(top, jnp.where(slot < live, scores[slot], -1e30))
            top = jnp.max(top, axis=1, keepdims=True) * EXPONENT_SCALE
            total = jnp.zeros((TILE, TILE), F32)
            result = jnp.zeros((TILE, 128), F32)
            for slot in range(KEEP):
                shift = top if slot == 0 else jnp.where(slot < live, top, 1e30)
                exponent = jnp.exp2(scores[slot] * EXPONENT_SCALE - shift)
                total = total + exponent
                result = result + jnp.dot(
                    exponent.astype(BF16), tile_v[head, picks[slot]], preferred_element_type=F32
                )
            total = jnp.sum(total, axis=1, keepdims=True)
            latent = latent + result * (1.0 / total)
        for half in range(2):
            base = half * 128
            packed[side, half] = jnp.where(
                packed_lane < 64, latent[base : base + 64], latent[base + 64 : base + 128]
            )

    def part_targets(owner):
        block = 2 * owner + core
        last = block // 7
        start = 1 - (block + 6) // 7
        own = part_sum.at[owner]
        return (
            (own, block, 32, 128, 0),
            (own.at[pl.ds(96, 32)], block + 1 - last, 160 * last, 32, 1 + last),
            (own.at[pl.ds(0, 32)], block - 1 + start, 160 * (1 - start), 32, 2 - start),
        )

    def to_sibling_part(owner):
        return remote(
            part_out.at[owner, 1 - core],
            sib_in.at[owner],
            sib_send.at[owner],
            sib_recv.at[owner],
            sp=sibling,
        )

    def one_chip(owner):
        place(got_q, 2 * owner, tile_q, 0)
        place(got_q, 2 * owner + 1, tile_q, 0)
        one_tile(owner, 0)
        one_tile(owner, 1)
        for half in range(2):
            pieces = []
            for row in range(4):
                for frame in range(2):
                    for side in range(2):
                        at = (frame * 4 + row) * 8
                        pieces.append(packed[side, half, at : at + 8])
            part_out[owner, half] = jnp.concatenate(pieces, axis=0).astype(BF16)
        exchange_parts = to_sibling_part(owner)
        exchange_parts.start()
        exchange_parts.wait_recv()
        part_sum[owner] = (
            part_out[owner, core].astype(F32) + sib_in[owner].astype(F32)
        ).astype(BF16)
        for kind, (source, target, at, size, region) in enumerate(part_targets(owner)):
            place_at = part_in.at[chip, pl.ds(pl.multiple_of(at, 32), size)]
            arrived = part_recv.at[chip, region]

            @pl.when(target != me)
            def _():
                remote(source, place_at, part_send.at[owner, kind], arrived, sp=target).start()

            @pl.when(target == me)
            def _():
                pltpu.make_async_copy(source, place_at, arrived).start()

    all_lanes = weights_out.at[:, :, lanes]
    to_sibling = remote(all_lanes, all_lanes, w_send.at[11], w_recv.at[11], sp=sibling)

    def chip_turn(turn, carry):
        owner = (
            (turn == 0) * chip + (turn == 1) * near + (turn == 2) * far + (turn == 3) * mirror
        )

        @pl.when(turn > 0)
        def _():
            for k in range(2):
                wait_block(2, got_q, owner * 2 + k)

        one_chip(owner)
        return carry

    wait_block(2, got_q, sibling)
    lax.fori_loop(0, 4, chip_turn, 0)
    for copy in x_sends:
        copy.wait()
    to_sibling.start()

    latent = jnp.zeros((192, 128), F32)
    for src in range(4):
        for region, (at, size) in enumerate(((32, 128), (0, 32), (160, 32))):
            rows = part_in.at[src, pl.ds(at, size)]
            pltpu.make_async_copy(rows, rows, part_recv.at[src, region]).wait()
        latent = latent + part_in[src].astype(F32)
    seg_latent[seg] = latent.astype(BF16)
    seg_copies = []
    for i, peer in enumerate(x_peers):
        copy = remote(
            seg_latent.at[seg], seg_latent.at[seg], seg_send.at[i], seg_recv.at[i], segment=peer
        )
        copy.start()
        seg_copies.append(copy)
    for copy in seg_copies:
        copy.wait()
    source = jnp.int32(0)
    for micro in range(1, 4):
        source = jnp.where(decode_slot[micro] == seg, micro, source)
    latent_out[...] = seg_latent[source]

    def drain(owner, carry):
        to_sibling_part(owner).wait_send()
        for kind, (source, target, at, size, region) in enumerate(part_targets(owner)):

            @pl.when(target != me)
            def _():
                remote(
                    source,
                    part_in.at[chip, pl.ds(0, size)],
                    part_send.at[owner, kind],
                    part_recv.at[chip, region],
                    sp=target,
                ).wait_send()

        return carry

    lax.fori_loop(0, 4, drain, 0)
    to_sibling.wait()
    for copy in sends:
        copy.wait_send()


def exchange(kept, counts, decode_slot, queries, keys, values, patch, piece):
    any_space = pl.BlockSpec(memory_space=pl.ANY)
    smem = pl.BlockSpec(memory_space=pltpu.SMEM)
    vmem = pl.BlockSpec(memory_space=pltpu.VMEM)
    return pl.pallas_call(
        exchange_kernel,
        out_shape=(
            jax.ShapeDtypeStruct((192, 128), BF16),
            jax.ShapeDtypeStruct((28, CH, CH), BF16),
        ),
        in_specs=[smem, smem, smem] + [any_space] * 5,
        out_specs=(vmem, any_space),
        scratch_shapes=[
            pltpu.VMEM((8, 256, 256), BF16),
            pltpu.VMEM((8, 256, 256), BF16),
            pltpu.VMEM((8, 256, 128), BF16),
            pltpu.VMEM((2, 2, TILE, HD), BF16),
            pltpu.VMEM((2, NT, TILE, HD), BF16),
            pltpu.VMEM((2, NT, TILE, 128), BF16),
            pltpu.VMEM((256, 256), BF16),
            pltpu.VMEM((64, HEADS * HD), BF16),
            pltpu.VMEM((256, HEADS * HD), BF16),
            pltpu.VMEM((8, 256, 128), BF16),
            pltpu.VMEM((2, 2, 64, 128), F32),
            pltpu.VMEM((4, 2, 128, 128), BF16),
            pltpu.VMEM((4, 128, 128), BF16),
            pltpu.VMEM((4, 128, 128), BF16),
            pltpu.VMEM((4, 192, 128), BF16),
            pltpu.VMEM((4, 192, 128), BF16),
            pltpu.SemaphoreType.DMA((3, 7)),
            pltpu.SemaphoreType.DMA((3, 8)),
            pltpu.SemaphoreType.DMA((4,)),
            pltpu.SemaphoreType.DMA((4,)),
            pltpu.SemaphoreType.DMA((4,)),
            pltpu.SemaphoreType.DMA((4, 3)),
            pltpu.SemaphoreType.DMA((4, 3)),
            pltpu.SemaphoreType.DMA((3,)),
            pltpu.SemaphoreType.DMA((3,)),
            pltpu.SemaphoreType.DMA,
            pltpu.SemaphoreType.DMA((13,)),
            pltpu.SemaphoreType.DMA((12,)),
        ],
        compiler_params=pltpu.CompilerParams(
            collective_id=0, has_side_effects=True, vmem_limit_bytes=60 << 20
        ),
        cost_estimate=pl.CostEstimate(
            flops=4 * 16 * 4 * 256 * 256 * 128, bytes_accessed=10 << 20, transcendentals=1 << 22
        ),
    )(kept, counts, decode_slot, queries, keys, values, patch, piece)


def slot_of(offset):
    return offset if offset < 21 else offset + 1


def decode_kernel(
    latent, first_kernel, weights, out, window, rows, first, act, weights_vmem, weight_sem
):
    me = lax.axis_index("sp")
    load = pltpu.make_async_copy(weights, weights_vmem, weight_sem)
    load.start()

    twice = (
        lax.broadcasted_iota(jnp.int32, (384, 192), 0) // 2
        == lax.broadcasted_iota(jnp.int32, (384, 192), 1)
    ).astype(BF16)
    doubled = jnp.dot(twice, latent[...], preferred_element_type=F32)
    column = lax.broadcasted_iota(jnp.int32, (384, 128), 0) % 32
    here = jnp.where(column % 2 == 0, doubled, pltpu.roll(doubled, 128 - LAT, axis=1))
    before = jnp.where(column == 0, here, pltpu.roll(here, 1, axis=0))
    after = jnp.where(column == 31, here, pltpu.roll(here, 383, axis=0))
    source_lane = lax.broadcasted_iota(jnp.int32, (384, 512), 0)
    target_lane = lax.broadcasted_iota(jnp.int32, (384, 512), 1)
    slot = target_lane % 128
    wanted = (slot // LAT) * 128 + (target_lane // 128) * 32 + slot % LAT
    pick = jnp.logical_and(slot < 48, source_lane == wanted).astype(BF16)
    joined = jnp.dot(
        jnp.concatenate([before, here, after], axis=1).astype(BF16),
        pick,
        preferred_element_type=F32,
    ).astype(BF16)
    for row in range(6):
        for frame_low in range(2):
            at = (row * 2 + frame_low) * 32
            for frame_high in range(2):
                for up in range(2):
                    lane = (frame_high * 2 + up) * 128
                    window[frame_high * 2 + frame_low, 2 * row + up] = joined[
                        at : at + 32, lane : lane + 128
                    ]

    @pl.when(me == 0)
    def _():
        window[:, 1] = window[:, 2]

    @pl.when(me == 7)
    def _():
        window[:, 10] = window[:, 9]

    for frame in range(4):
        rows[frame] = jnp.concatenate(
            [window[frame, row : row + 10, :, 0:48].reshape(320, 48) for row in range(3)], axis=1
        )
    wide_column = lax.broadcasted_iota(jnp.int32, (320, CH), 0) % 32
    for frame in range(4):
        total = jnp.zeros((320, CH), F32)
        for time in range(3):
            total = total + jnp.dot(
                rows[max(frame + time - 2, 0)],
                first_kernel[time * 144 : time * 144 + 144],
                preferred_element_type=F32,
            )
        rounded = (total * VAE_SCALE).astype(BF16)
        first[frame * 256 : frame * 256 + 256] = rounded[32:288]
        wide = rounded.astype(F32)
        wide = (wide / (1.0 + jnp.exp(-wide))).astype(BF16).astype(F32)
        before = jnp.where(wide_column == 0, wide, pltpu.roll(wide, 1, axis=0))
        after = jnp.where(wide_column == 31, wide, pltpu.roll(wide, 319, axis=0))
        for place, part in enumerate((before, wide, after)):
            part = part.reshape(10, 32, CH).astype(BF16)
            act[frame + 2, :, :, place * CH : place * CH + CH] = part
            if frame == 0:
                act[0, :, :, place * CH : place * CH + CH] = part
                act[1, :, :, place * CH : place * CH + CH] = part

    @pl.when(me == 0)
    def _():
        act[:, 0] = act[:, 1]

    @pl.when(me == 7)
    def _():
        act[:, 9] = act[:, 8]

    load.wait()
    for part in range(2):
        total = first[part * 512 : part * 512 + 512].astype(F32)
        for time in range(3):
            for row in range(3):
                slot = slot_of((time * 3 + row) * 3)
                block = act[part * 2 + time : part * 2 + time + 2, row : row + 8]
                total = total + jnp.dot(
                    block.reshape(512, 3 * CH),
                    weights_vmem[slot : slot + 3].reshape(3 * CH, CH),
                    preferred_element_type=F32,
                )
        out[part * 512 : part * 512 + 512] = total.astype(BF16)


def decode(latent, first_kernel, weights):
    vmem = pl.BlockSpec(memory_space=pltpu.VMEM)
    return pl.pallas_call(
        decode_kernel,
        out_shape=jax.ShapeDtypeStruct((1024, CH), BF16),
        in_specs=[vmem, vmem, pl.BlockSpec(memory_space=pl.ANY)],
        out_specs=vmem,
        scratch_shapes=[
            pltpu.VMEM((4, 12, 32, 128), BF16),
            pltpu.VMEM((4, 320, 144), BF16),
            pltpu.VMEM((1024, CH), BF16),
            pltpu.VMEM((6, 10, 32, 3 * CH), BF16),
            pltpu.VMEM((28, CH, CH), BF16),
            pltpu.SemaphoreType.DMA,
        ],
        compiler_params=pltpu.CompilerParams(vmem_limit_bytes=60 << 20),
        cost_estimate=pl.CostEstimate(
            flops=2 * 1024 * 27 * 256 * 256, bytes_accessed=5 << 20, transcendentals=1 << 19
        ),
    )(latent, first_kernel, weights)


def local(
    queries,
    key_states,
    value_states,
    kept_tiles,
    kept_counts,
    patch_weight,
    decode_slot,
    first_kernel,
    second_kernel,
):
    latent, weights = exchange(
        kept_tiles.transpose(1, 2, 0),
        kept_counts.transpose(1, 0),
        decode_slot,
        queries.reshape(256, HEADS * HD),
        key_states.reshape(256, HEADS * HD),
        value_states.reshape(256, HEADS * HD),
        patch_weight.transpose(1, 0),
        second_kernel,
    )
    decoded = decode(latent, first_kernel.reshape(27 * LAT, CH), weights)
    return decoded.reshape(1, 1, 4, 8, 32, CH)


def solution(mesh):
    tokens = P("segment", "grp", None, "sp", None, None)
    return jax.shard_map(
        local,
        mesh=mesh,
        in_specs=(tokens, tokens, tokens, P(), P(), P(), P(), P(), P(None, "grp", None)),
        out_specs=tokens,
        check_vma=False,
    )
```

```python
import functools
import math

import jax
import jax.numpy as jnp
from jax import lax
from jax.experimental import pallas as pl
from jax.experimental.pallas import tpu as pltpu
from jax.sharding import PartitionSpec as P

HEADS = 16
HD = 128
LAT = 16
CH = 256
NT = 8
KEEP = 4
TILE = 256
VAE_SCALE = 1.0 / 0.476986
MESH = pl.DeviceIdType.MESH
BF16 = jnp.bfloat16
F32 = jnp.float32
EXPONENT_SCALE = HD**-0.5 * math.log2(math.e)


def remote(src, dst, send_sem, recv_sem, **where):
    return pltpu.make_async_remote_copy(
        src_ref=src,
        dst_ref=dst,
        send_sem=send_sem,
        recv_sem=recv_sem,
        device_id=where,
        device_id_type=MESH,
    )


def exchange_kernel(
    kept,
    counts,
    decode_slot,
    queries,
    keys,
    values,
    patch,
    piece,
    latent_out,
    weights_out,
    got_q,
    got_k,
    got_v,
    tile_q,
    tile_k,
    tile_v,
    order,
    patch_all,
    own_values,
    projected,
    packed,
    part_out,
    sib_in,
    part_sum,
    part_in,
    seg_latent,
    send_sem,
    recv_sem,
    local_sem,
    sib_send,
    sib_recv,
    part_send,
    part_recv,
    seg_send,
    seg_recv,
    w_local,
    w_send,
    w_recv,
):
    me = lax.axis_index("sp")
    seg = lax.axis_index("segment")
    grp = lax.axis_index("grp")
    chip = me // 2
    core = me % 2
    sibling = chip * 2 + 1 - core
    far = (chip + 2) % 4
    mirror = 3 - chip
    near = chip + 1 - 2 * (chip % 2)
    peers = [
        mirror * 2 + core,
        mirror * 2 + 1 - core,
        far * 2 + core,
        far * 2 + 1 - core,
        near * 2 + core,
        near * 2 + 1 - core,
        sibling,
    ]
    z_partner = grp + 1 - 2 * (grp % 2)
    y_peers = [(grp + 2 * step) % 16 for step in range(1, 8)]
    x_peers = [(seg + step) % 4 for step in range(1, 4)]

    barrier = pltpu.get_barrier_semaphore()
    for peer in peers:
        pl.semaphore_signal(barrier, inc=1, device_id={"sp": peer}, device_id_type=MESH)
    for peer in x_peers:
        pl.semaphore_signal(barrier, inc=1, device_id={"segment": peer}, device_id_type=MESH)
    for peer in y_peers:
        pl.semaphore_signal(barrier, inc=1, device_id={"grp": peer}, device_id_type=MESH)
    at_border = chip % 3 == 0
    source_chip = 3 * (1 - chip // 2)
    pl.semaphore_signal(
        barrier,
        inc=1,
        device_id={"grp": z_partner, "sp": source_chip * 2 + core},
        device_id_type=MESH,
    )
    pl.semaphore_wait(barrier, 17 + 2 * at_border.astype(jnp.int32))

    quarter = seg * 7
    taps = pl.ds(quarter, 7)
    lanes = pl.ds(pl.multiple_of(core * 128, 128), 128)
    own_part = piece.at[pl.ds(quarter - seg // 3, 7), :, lanes]
    own_rows = pl.ds(pl.multiple_of(grp * 16, 16), 16)
    own_place = weights_out.at[taps, own_rows, lanes]
    w_keep = pltpu.make_async_copy(own_part, own_place, w_local)
    w_keep.start()
    beyond = mirror + 1 - 2 * (mirror % 2)
    w_cross = [
        remote(
            own_part,
            own_place,
            w_send.at[place],
            w_recv.at[0],
            grp=z_partner,
            sp=target * 2 + core,
        )
        for place, target in ((0, mirror), (12, beyond))
    ]

    @pl.when(at_border)
    def _():
        for copy in w_cross:
            copy.start()

    sends = []

    def send(a, source, target):
        for i, peer in enumerate(peers):
            copy = remote(source(peer), target.at[me], send_sem.at[a, i], recv_sem.at[a, me], sp=peer)
            copy.start()
            sends.append(copy)

    def columns_of(ref):
        return lambda peer: ref.at[:, pl.ds(pl.multiple_of(peer * 256, 256), 256)]

    load_values = pltpu.make_async_copy(values, own_values, local_sem.at[0])
    load_values.start()
    load_patch = pltpu.make_async_copy(patch, patch_all, local_sem.at[1])
    load_patch.start()
    send(0, columns_of(keys), got_k)
    keep_keys = pltpu.make_async_copy(columns_of(keys)(me), got_k.at[me], local_sem.at[2])
    keep_keys.start()
    keep_queries = pltpu.make_async_copy(columns_of(queries)(me), got_q.at[me], local_sem.at[3])
    keep_queries.start()

    load_values.wait()
    load_patch.wait()
    patch_lane = lax.broadcasted_iota(jnp.int32, (64, 256), 1)

    def project(peer, carry):
        columns = pl.ds(pl.multiple_of(peer * 256, 256), 256)
        weight = patch_all[:, columns].astype(F32)
        weight = jnp.concatenate(
            [jnp.where(patch_lane < HD, weight, 0.0), jnp.where(patch_lane < HD, 0.0, weight)],
            axis=0,
        ).astype(BF16)
        projected[peer] = lax.dot_general(
            own_values[:, columns],
            weight,
            (((1,), (1,)), ((), ())),
            preferred_element_type=F32,
        ).astype(BF16)
        return carry

    lax.fori_loop(0, 8, project, 0)
    send(1, lambda peer: projected.at[peer], got_v)
    got_v[me] = projected[me]
    send(2, columns_of(queries), got_q)

    w_keep.wait()
    w_cross[0].wait_recv()

    @pl.when(at_border)
    def _():
        for copy in w_cross:
            copy.wait_send()

    pair_rows = pl.ds(pl.multiple_of((grp // 2) * 32, 32), 32)
    y_sends = []
    for i, peer in enumerate(y_peers):
        block = weights_out.at[taps, pair_rows, lanes]
        copy = remote(block, block, w_send.at[1 + i], w_recv.at[1 + i], grp=peer)
        copy.start()
        y_sends.append(copy)
    keep_keys.wait()
    keep_queries.wait()
    def wait_block(a, target, src):
        remote(
            target.at[src], target.at[src], send_sem.at[a, 0], recv_sem.at[a, src], sp=sibling
        ).wait_recv()

    to_row = lax.broadcasted_iota(jnp.int32, (256, 256), 0)
    from_row = lax.broadcasted_iota(jnp.int32, (256, 256), 1)
    wanted = ((to_row % 128) // 8) * 16 + (to_row // 128) * 8 + to_row % 8
    order[...] = (from_row == wanted).astype(BF16)

    def place(got, src, tiles, first_tile):
        block = jnp.dot(order[...], got[src], preferred_element_type=F32).astype(BF16)
        rows = pl.ds(pl.multiple_of((src % 2) * 128, 128), 128)
        for head in range(2):
            for side in range(2):
                tiles[head, first_tile + side, rows] = block[
                    side * 128 : side * 128 + 128, head * 128 : head * 128 + 128
                ]

    value_lane = lax.broadcasted_iota(jnp.int32, (256, 128), 1)

    def place_keys(src):
        place(got_k, src, tile_k, 2 * (src // 2))
        block = jnp.dot(order[...], got_v[src], preferred_element_type=F32)
        turned = pltpu.roll(block, 64, axis=1)
        rows = pl.ds(pl.multiple_of((src % 2) * 128, 128), 128)
        for head, (left, right) in enumerate(((block, turned), (turned, block))):
            both = jnp.where(value_lane < 64, left, right).astype(BF16)
            for side in range(2):
                tile_v[head, 2 * (src // 2) + side, rows] = both[side * 128 : side * 128 + 128]

    place_keys(me)
    for peer in (peers[6], peers[4], peers[5]):
        wait_block(0, got_k, peer)
        wait_block(1, got_v, peer)
        place_keys(peer)

    for copy in y_sends:
        copy.wait()
    x_sends = []
    own_quarter = weights_out.at[taps, :, lanes]
    for i, peer in enumerate(x_peers):
        copy = remote(own_quarter, own_quarter, w_send.at[8 + i], w_recv.at[8 + i], segment=peer)
        copy.start()
        x_sends.append(copy)

    for peer in peers[:4]:
        wait_block(0, got_k, peer)
        wait_block(1, got_v, peer)
        place_keys(peer)

    head_base = me * 2
    packed_lane = lax.broadcasted_iota(jnp.int32, (64, 128), 1)

    def one_tile(owner, side):
        tile = 2 * owner + side
        latent = jnp.zeros((TILE, 128), F32)
        for head in range(2):
            query = tile_q[head, side]
            live = counts[tile, head_base + head]
            scores, picks = [], []
            for slot in range(KEEP):
                pick = kept[tile, slot, head_base + head]
                picks.append(pick)
                scores.append(
                    lax.dot_general(
                        query,
                        tile_k[head, pick],
                        (((1,), (1,)), ((), ())),
                        preferred_element_type=F32,
                    )
                )
            top = scores[0]
            for slot in range(1, KEEP):
                top = jnp.maximum(top, jnp.where(slot < live, scores[slot], -1e30))
            top = jnp.max(top, axis=1, keepdims=True) * EXPONENT_SCALE
            total = jnp.zeros((TILE, TILE), F32)
            result = jnp.zeros((TILE, 128), F32)
            for slot in range(KEEP):
                shift = top if slot == 0 else jnp.where(slot < live, top, 1e30)
                exponent = jnp.exp2(scores[slot] * EXPONENT_SCALE - shift)
                total = total + exponent
                result = result + jnp.dot(
                    exponent.astype(BF16), tile_v[head, picks[slot]], preferred_element_type=F32
                )
            total = jnp.sum(total, axis=1, keepdims=True)
            latent = latent + result * (1.0 / total)
        for half in range(2):
            base = half * 128
            packed[side, half] = jnp.where(
                packed_lane < 64, latent[base : base + 64], latent[base + 64 : base + 128]
            )

    def part_targets(owner):
        block = 2 * owner + core
        last = block // 7
        start = 1 - (block + 6) // 7
        own = part_sum.at[owner]
        return (
            (own, block, 32, 128, 0),
            (own.at[pl.ds(96, 32)], block + 1 - last, 160 * last, 32, 1 + last),
            (own.at[pl.ds(0, 32)], block - 1 + start, 160 * (1 - start), 32, 2 - start),
        )

    def to_sibling_part(owner):
        return remote(
            part_out.at[owner, 1 - core],
            sib_in.at[owner],
            sib_send.at[owner],
            sib_recv.at[owner],
            sp=sibling,
        )

    def one_chip(owner):
        place(got_q, 2 * owner, tile_q, 0)
        place(got_q, 2 * owner + 1, tile_q, 0)
        one_tile(owner, 0)
        one_tile(owner, 1)
        for half in range(2):
            pieces = []
            for row in range(4):
                for frame in range(2):
                    for side in range(2):
                        at = (frame * 4 + row) * 8
                        pieces.append(packed[side, half, at : at + 8])
            part_out[owner, half] = jnp.concatenate(pieces, axis=0).astype(BF16)
        exchange_parts = to_sibling_part(owner)
        exchange_parts.start()
        exchange_parts.wait_recv()
        part_sum[owner] = (
            part_out[owner, core].astype(F32) + sib_in[owner].astype(F32)
        ).astype(BF16)
        for kind, (source, target, at, size, region) in enumerate(part_targets(owner)):
            place_at = part_in.at[chip, pl.ds(pl.multiple_of(at, 32), size)]
            arrived = part_recv.at[chip, region]

            @pl.when(target != me)
            def _():
                remote(source, place_at, part_send.at[owner, kind], arrived, sp=target).start()

            @pl.when(target == me)
            def _():
                pltpu.make_async_copy(source, place_at, arrived).start()

    all_lanes = weights_out.at[:, :, lanes]
    to_sibling = remote(all_lanes, all_lanes, w_send.at[11], w_recv.at[11], sp=sibling)

    def chip_turn(turn, carry):
        owner = (
            (turn == 0) * chip + (turn == 1) * near + (turn == 2) * mirror + (turn == 3) * far
        )

        @pl.when(turn > 0)
        def _():
            for k in range(2):
                wait_block(2, got_q, owner * 2 + k)

        one_chip(owner)
        return carry

    wait_block(2, got_q, sibling)
    lax.fori_loop(0, 4, chip_turn, 0)
    for copy in x_sends:
        copy.wait()
    to_sibling.start()

    latent = jnp.zeros((192, 128), F32)
    for src in range(4):
        for region, (at, size) in enumerate(((32, 128), (0, 32), (160, 32))):
            rows = part_in.at[src, pl.ds(at, size)]
            pltpu.make_async_copy(rows, rows, part_recv.at[src, region]).wait()
        latent = latent + part_in[src].astype(F32)
    seg_latent[seg] = latent.astype(BF16)
    seg_copies = []
    for i, peer in enumerate(x_peers):
        copy = remote(
            seg_latent.at[seg], seg_latent.at[seg], seg_send.at[i], seg_recv.at[i], segment=peer
        )
        copy.start()
        seg_copies.append(copy)
    for copy in seg_copies:
        copy.wait()
    source = jnp.int32(0)
    for micro in range(1, 4):
        source = jnp.where(decode_slot[micro] == seg, micro, source)
    latent_out[...] = seg_latent[source]

    def drain(owner, carry):
        to_sibling_part(owner).wait_send()
        for kind, (source, target, at, size, region) in enumerate(part_targets(owner)):

            @pl.when(target != me)
            def _():
                remote(
                    source,
                    part_in.at[chip, pl.ds(0, size)],
                    part_send.at[owner, kind],
                    part_recv.at[chip, region],
                    sp=target,
                ).wait_send()

        return carry

    lax.fori_loop(0, 4, drain, 0)
    to_sibling.wait()
    for copy in sends:
        copy.wait_send()


def exchange(kept, counts, decode_slot, queries, keys, values, patch, piece):
    any_space = pl.BlockSpec(memory_space=pl.ANY)
    smem = pl.BlockSpec(memory_space=pltpu.SMEM)
    vmem = pl.BlockSpec(memory_space=pltpu.VMEM)
    return pl.pallas_call(
        exchange_kernel,
        out_shape=(
            jax.ShapeDtypeStruct((192, 128), BF16),
            jax.ShapeDtypeStruct((28, CH, CH), BF16),
        ),
        in_specs=[smem, smem, smem] + [any_space] * 5,
        out_specs=(vmem, any_space),
        scratch_shapes=[
            pltpu.VMEM((8, 256, 256), BF16),
            pltpu.VMEM((8, 256, 256), BF16),
            pltpu.VMEM((8, 256, 128), BF16),
            pltpu.VMEM((2, 2, TILE, HD), BF16),
            pltpu.VMEM((2, NT, TILE, HD), BF16),
            pltpu.VMEM((2, NT, TILE, 128), BF16),
            pltpu.VMEM((256, 256), BF16),
            pltpu.VMEM((64, HEADS * HD), BF16),
            pltpu.VMEM((256, HEADS * HD), BF16),
            pltpu.VMEM((8, 256, 128), BF16),
            pltpu.VMEM((2, 2, 64, 128), F32),
            pltpu.VMEM((4, 2, 128, 128), BF16),
            pltpu.VMEM((4, 128, 128), BF16),
            pltpu.VMEM((4, 128, 128), BF16),
            pltpu.VMEM((4, 192, 128), BF16),
            pltpu.VMEM((4, 192, 128), BF16),
            pltpu.SemaphoreType.DMA((3, 7)),
            pltpu.SemaphoreType.DMA((3, 8)),
            pltpu.SemaphoreType.DMA((4,)),
            pltpu.SemaphoreType.DMA((4,)),
            pltpu.SemaphoreType.DMA((4,)),
            pltpu.SemaphoreType.DMA((4, 3)),
            pltpu.SemaphoreType.DMA((4, 3)),
            pltpu.SemaphoreType.DMA((3,)),
            pltpu.SemaphoreType.DMA((3,)),
            pltpu.SemaphoreType.DMA,
            pltpu.SemaphoreType.DMA((13,)),
            pltpu.SemaphoreType.DMA((12,)),
        ],
        compiler_params=pltpu.CompilerParams(
            collective_id=0, has_side_effects=True, vmem_limit_bytes=60 << 20
        ),
        cost_estimate=pl.CostEstimate(
            flops=4 * 16 * 4 * 256 * 256 * 128, bytes_accessed=10 << 20, transcendentals=1 << 22
        ),
    )(kept, counts, decode_slot, queries, keys, values, patch, piece)


def slot_of(offset):
    return offset if offset < 21 else offset + 1


def decode_kernel(
    latent, first_kernel, weights, out, window, rows, first, act, weights_vmem, weight_sem
):
    me = lax.axis_index("sp")
    load = pltpu.make_async_copy(weights, weights_vmem, weight_sem)
    load.start()

    twice = (
        lax.broadcasted_iota(jnp.int32, (384, 192), 0) // 2
        == lax.broadcasted_iota(jnp.int32, (384, 192), 1)
    ).astype(BF16)
    doubled = jnp.dot(twice, latent[...], preferred_element_type=F32)
    column = lax.broadcasted_iota(jnp.int32, (384, 128), 0) % 32
    here = jnp.where(column % 2 == 0, doubled, pltpu.roll(doubled, 128 - LAT, axis=1))
    before = jnp.where(column == 0, here, pltpu.roll(here, 1, axis=0))
    after = jnp.where(column == 31, here, pltpu.roll(here, 383, axis=0))
    source_lane = lax.broadcasted_iota(jnp.int32, (384, 512), 0)
    target_lane = lax.broadcasted_iota(jnp.int32, (384, 512), 1)
    slot = target_lane % 128
    wanted = (slot // LAT) * 128 + (target_lane // 128) * 32 + slot % LAT
    pick = jnp.logical_and(slot < 48, source_lane == wanted).astype(BF16)
    joined = jnp.dot(
        jnp.concatenate([before, here, after], axis=1).astype(BF16),
        pick,
        preferred_element_type=F32,
    ).astype(BF16)
    for row in range(6):
        for frame_low in range(2):
            at = (row * 2 + frame_low) * 32
            for frame_high in range(2):
                for up in range(2):
                    lane = (frame_high * 2 + up) * 128
                    window[frame_high * 2 + frame_low, 2 * row + up] = joined[
                        at : at + 32, lane : lane + 128
                    ]

    @pl.when(me == 0)
    def _():
        window[:, 1] = window[:, 2]

    @pl.when(me == 7)
    def _():
        window[:, 10] = window[:, 9]

    for frame in range(4):
        rows[frame] = jnp.concatenate(
            [window[frame, row : row + 10, :, 0:48].reshape(320, 48) for row in range(3)], axis=1
        )
    wide_column = lax.broadcasted_iota(jnp.int32, (320, CH), 0) % 32
    for frame in range(4):
        total = jnp.zeros((320, CH), F32)
        for time in range(3):
            total = total + jnp.dot(
                rows[max(frame + time - 2, 0)],
                first_kernel[time * 144 : time * 144 + 144],
                preferred_element_type=F32,
            )
        rounded = (total * VAE_SCALE).astype(BF16)
        first[frame * 256 : frame * 256 + 256] = rounded[32:288]
        wide = rounded.astype(F32)
        wide = (wide / (1.0 + jnp.exp(-wide))).astype(BF16).astype(F32)
        before = jnp.where(wide_column == 0, wide, pltpu.roll(wide, 1, axis=0))
        after = jnp.where(wide_column == 31, wide, pltpu.roll(wide, 319, axis=0))
        for place, part in enumerate((before, wide, after)):
            part = part.reshape(10, 32, CH).astype(BF16)
            act[frame + 2, :, :, place * CH : place * CH + CH] = part
            if frame == 0:
                act[0, :, :, place * CH : place * CH + CH] = part
                act[1, :, :, place * CH : place * CH + CH] = part

    @pl.when(me == 0)
    def _():
        act[:, 0] = act[:, 1]

    @pl.when(me == 7)
    def _():
        act[:, 9] = act[:, 8]

    load.wait()
    for part in range(2):
        total = first[part * 512 : part * 512 + 512].astype(F32)
        for time in range(3):
            for row in range(3):
                slot = slot_of((time * 3 + row) * 3)
                block = act[part * 2 + time : part * 2 + time + 2, row : row + 8]
                total = total + jnp.dot(
                    block.reshape(512, 3 * CH),
                    weights_vmem[slot : slot + 3].reshape(3 * CH, CH),
                    preferred_element_type=F32,
                )
        out[part * 512 : part * 512 + 512] = total.astype(BF16)


def decode(latent, first_kernel, weights):
    vmem = pl.BlockSpec(memory_space=pltpu.VMEM)
    return pl.pallas_call(
        decode_kernel,
        out_shape=jax.ShapeDtypeStruct((1024, CH), BF16),
        in_specs=[vmem, vmem, pl.BlockSpec(memory_space=pl.ANY)],
        out_specs=vmem,
        scratch_shapes=[
            pltpu.VMEM((4, 12, 32, 128), BF16),
            pltpu.VMEM((4, 320, 144), BF16),
            pltpu.VMEM((1024, CH), BF16),
            pltpu.VMEM((6, 10, 32, 3 * CH), BF16),
            pltpu.VMEM((28, CH, CH), BF16),
            pltpu.SemaphoreType.DMA,
        ],
        compiler_params=pltpu.CompilerParams(vmem_limit_bytes=60 << 20),
        cost_estimate=pl.CostEstimate(
            flops=2 * 1024 * 27 * 256 * 256, bytes_accessed=5 << 20, transcendentals=1 << 19
        ),
    )(latent, first_kernel, weights)


def local(
    queries,
    key_states,
    value_states,
    kept_tiles,
    kept_counts,
    patch_weight,
    decode_slot,
    first_kernel,
    second_kernel,
):
    latent, weights = exchange(
        kept_tiles.transpose(1, 2, 0),
        kept_counts.transpose(1, 0),
        decode_slot,
        queries.reshape(256, HEADS * HD),
        key_states.reshape(256, HEADS * HD),
        value_states.reshape(256, HEADS * HD),
        patch_weight.transpose(1, 0),
        second_kernel,
    )
    decoded = decode(latent, first_kernel.reshape(27 * LAT, CH), weights)
    return decoded.reshape(1, 1, 4, 8, 32, CH)


def solution(mesh):
    tokens = P("segment", "grp", None, "sp", None, None)
    return jax.shard_map(
        local,
        mesh=mesh,
        in_specs=(tokens, tokens, tokens, P(), P(), P(), P(), P(), P(None, "grp", None)),
        out_specs=tokens,
        check_vma=False,
    )
```
